512 devices in a mesh: ens: 4 (over x), lat: 8 (over z_lo), lon: 16 (over z_hi, y, core).
Axes of the slice: x: 4, y: 4, z: 16 (z_hi: 2, z_lo: 8; z = z_hi * 8 + z_lo), core: 2. Of those that a mesh axis runs over, the one named last changes fastest.
Arguments:
- features: bfloat16 [4, 128, 128, 2048], P('ens', None, 'lat', 'lon'), may hold values from -21 to 21
- conv_weight: bfloat16 [128, 9, 128], replicated, may hold values from -0.1875 to 0.1875
- conv_bias: float32 [128], replicated, may hold values from -3 to 3
- out_weight: bfloat16 [69, 128], replicated, may hold values from -0.5 to 0.5
- out_bias: float32 [69], replicated, may hold values from -3 to 3
- var_weight: float32 [69], replicated, may hold values from 0.2 to 2
- target: float32 [69, 128, 2048], P(None, 'lat', 'lon'), may hold values from -6 to 6
Outputs:
- grad_features: bfloat16 [4, 128, 128, 2048], P('ens', None, 'lat', 'lon')
- grad_weight: float32 [128, 9, 128], P('lon')
The draws below stay inside these ranges and needn't reach their ends.
All inputs are finite; a program needn't handle non-finite values.
Results may differ from the reference program's by a relative error of at most 0.038.
Values may be sent and summed in bfloat16 or wider, within the bound.
No kernel may reach another device: no remote copies, remote signals or barrier semaphores. Data moves between devices by JAX's collectives and lax.ppermute only.
A program may use at most 64 MiB of HBM per device.

```python
import math
import jax
import jax.numpy as jnp
from jax import lax

C = 128
V = 69
ROWS_DEV = 16
COLS_DEV = 128
MEMBERS = 4
NLAT = 128
NLON = 2048


def draw_features(key, part):
    key = jax.random.fold_in(key, 11)
    base_key, group_key, loop_key = jax.random.split(key, 3)
    band_count = NLAT // ROWS_DEV
    loop_count = NLON // COLS_DEV
    group_count = MEMBERS * band_count
    base = jnp.clip(jax.random.normal(base_key, (MEMBERS, C, NLAT, NLON), jnp.float32), -3.5, 3.5)
    group_perm = jax.random.permutation(group_key, group_count)
    loop_perm = jax.random.permutation(loop_key, loop_count)
    member_index = jnp.arange(MEMBERS)[:, None, None, None]
    channel_index = jnp.arange(C)[None, :, None, None]
    band_index = (jnp.arange(NLAT) // ROWS_DEV)[None, None, :, None]
    loop_index = (jnp.arange(NLON) // COLS_DEV)[None, None, None, :]
    group_hot = group_perm[member_index * band_count + band_index] == channel_index // (C // group_count)
    loop_hot = loop_perm[loop_index] == channel_index // (C // loop_count)
    scale = 1.0 + 3.0 * group_hot.astype(jnp.float32) + 2.0 * loop_hot.astype(jnp.float32)
    return (base * scale).astype(jnp.bfloat16)


def block_levels(key, extent, cuts, smallest, high):
    loudness = 1.0
    for dim, blocks in cuts:
        heights = jax.random.uniform(jax.random.fold_in(jax.random.fold_in(key, 6), dim), (blocks,), jnp.float32, smallest / len(cuts), high / len(cuts))
        loudness = loudness * jnp.repeat(jnp.exp(heights), extent[dim] // blocks).reshape((-1,) + (1,) * (len(extent) - 1 - dim))
    return loudness


def noise(own_key, extent, deviation, reach, cuts=(), dtype=jnp.bfloat16):
    drawn = jax.random.normal(own_key, extent, jnp.float32) * deviation
    if len(cuts) > 0:
        drawn = block_levels(own_key, extent, cuts, -0.22, 0.18) * drawn
    return jnp.clip(drawn, min=-reach, max=reach).astype(dtype)


def setup_inputs(seed: int = 0) -> dict:
    key_of = jax.random.split(jax.random.key(seed), 8)
    return {
        "features": draw_features(jax.random.fold_in(key_of[7], 71), 0),
        "conv_weight": noise(key_of[1], (C, 9, C), (9 * C) ** -0.5, 0.1875),
        "conv_bias": noise(key_of[2], (C,), 0.5, 3.0, (), jnp.float32),
        "out_weight": noise(key_of[3], (V, C), C ** -0.5, 0.5),
        "out_bias": noise(key_of[4], (V,), 0.5, 3.0, (), jnp.float32),
        "var_weight": jnp.clip(jnp.exp(jax.random.uniform(key_of[5], (V,), jnp.float32, math.log(0.2), math.log(2.0))), 0.2, 2.0),
        "target": noise(key_of[6], (V, NLAT, NLON), 1.0, 6.0, ((1, 8), (2, 16)), jnp.float32),
    }


smoothing = 0.1

def tap_offsets():
    return [(tap_index, tap_index // 3 - 1, tap_index % 3 - 1) for tap_index in range(9)]

def pad_pole(hidden_field):
    half_turn = NLON // 2
    north_row = jnp.roll(hidden_field[:, :1], half_turn, axis=2)
    south_row = jnp.roll(hidden_field[:, -1:], half_turn, axis=2)
    with_rows = jnp.concatenate([north_row, hidden_field, south_row], axis=1)
    return jnp.concatenate([with_rows[:, :, -1:], with_rows, with_rows[:, :, :1]], axis=2)

def forward(hidden_field, conv_weight, conv_bias):
    padded = pad_pole(hidden_field)
    pre_act = jnp.zeros((C, NLAT, NLON), jnp.float32) + conv_bias[:, None, None].astype(jnp.float32)
    for tap_index, shift_row, shift_col in tap_offsets():
        tap_slice = padded[:, 1 + shift_row:1 + shift_row + NLAT, 1 + shift_col:1 + shift_col + NLON]
        pre_act = pre_act + jnp.einsum('io,irc->orc', conv_weight[:, tap_index, :].astype(jnp.float32), tap_slice.astype(jnp.float32))
    return (padded, pre_act)

def member_grad(own_values, others, truth_rows, var_weight, members):
    differences = own_values[None] - others
    pair_term = lax.optimization_barrier(jnp.sum(differences / jnp.sqrt(differences * differences + smoothing * smoothing), axis=0))
    misfit = own_values - truth_rows
    fit_term = misfit / jnp.sqrt(misfit * misfit + smoothing * smoothing)
    scaled = var_weight[:, None, None] * (fit_term / members - pair_term / (members * (members - 1)))
    return scaled.astype(jnp.bfloat16)

def reference(features, conv_weight, conv_bias, out_weight, out_bias, var_weight, target):
    outputs = []
    for member in range(MEMBERS):
        padded, pre_act = forward(features[member], conv_weight, conv_bias)
        active = (pre_act * jax.nn.sigmoid(pre_act)).astype(jnp.bfloat16)
        result = jnp.dot(out_weight, active.reshape(C, -1), preferred_element_type=jnp.float32).reshape(V, NLAT, NLON)
        outputs.append((result + out_bias[:, None, None]).astype(jnp.bfloat16))
    ensemble = jnp.stack(outputs).astype(jnp.float32)
    grads = []
    weight_sum = jnp.zeros((C, 9, C), jnp.float32)
    for member in range(MEMBERS):
        padded, pre_act = forward(features[member], conv_weight, conv_bias)
        grad_out = member_grad(ensemble[member], ensemble, target, var_weight, MEMBERS)
        grad_act = jnp.einsum('vc,vrw->crw', out_weight.astype(jnp.float32), grad_out.astype(jnp.float32))
        sigmoid_z = jax.nn.sigmoid(pre_act)
        grad_pre = (grad_act * sigmoid_z * (1.0 + pre_act * (1.0 - sigmoid_z))).astype(jnp.bfloat16)
        grad_pad = jnp.zeros((C, NLAT + 2, NLON + 2), jnp.float32)
        weight_terms = []
        for tap_index, shift_row, shift_col in tap_offsets():
            tap_slice = padded[:, 1 + shift_row:1 + shift_row + NLAT, 1 + shift_col:1 + shift_col + NLON]
            weight_terms.append(jnp.einsum('irc,orc->io', tap_slice.astype(jnp.float32), grad_pre.astype(jnp.float32)))
            contrib = jnp.einsum('io,orc->irc', conv_weight[:, tap_index, :].astype(jnp.float32), grad_pre.astype(jnp.float32))
            grad_pad = grad_pad.at[:, 1 + shift_row:1 + shift_row + NLAT, 1 + shift_col:1 + shift_col + NLON].add(contrib)
        weight_sum = weight_sum + jnp.stack(weight_terms, axis=1)
        inner_grad = grad_pad[:, :, 1:-1]
        inner_grad = inner_grad.at[:, :, 0].add(grad_pad[:, :, -1])
        inner_grad = inner_grad.at[:, :, -1].add(grad_pad[:, :, 0])
        core_grad = inner_grad[:, 1:-1]
        core_grad = core_grad.at[:, 0].add(jnp.roll(inner_grad[:, 0], NLON // 2, axis=1))
        core_grad = core_grad.at[:, -1].add(jnp.roll(inner_grad[:, -1], NLON // 2, axis=1))
        grads.append(core_grad.astype(jnp.bfloat16))
    return (jnp.stack(grads), weight_sum / math.sqrt(MEMBERS * NLAT * NLON))
```

```python
import functools
import math

import jax
import jax.numpy as jnp
from jax import lax
from jax.experimental import pallas as pl
from jax.experimental.pallas import tpu as pltpu
from jax.sharding import PartitionSpec as P

smoothing = 0.1
LANES = 128


def dot(a, b, dims=(((1,), (0,)), ((), ()))):
    return lax.dot_general(a, b, dims, preferred_element_type=jnp.float32)


def forward_kernel(rows, x_ref, north_ref, south_ref, left_ref, right_ref, w_ref, b_ref, ow_ref, ob_ref,
                   out_ref, slope_ref, x3_ref):
    channels = x_ref.shape[0]
    lane = lax.broadcasted_iota(jnp.int32, (channels, LANES), 1)
    left_cols = left_ref[...].astype(jnp.float32)
    right_cols = right_ref[...].astype(jnp.float32)
    north = north_ref[...].astype(jnp.float32)
    south = south_ref[...].astype(jnp.float32)
    for row in range(rows + 2):
        if row == 0:
            block, before, after = north[:, :LANES], north[:, LANES : LANES + 1], north[:, LANES + 1 :]
        elif row == rows + 1:
            block, before, after = south[:, :LANES], south[:, LANES : LANES + 1], south[:, LANES + 1 :]
        else:
            block = x_ref[:, (row - 1) * LANES : row * LANES].astype(jnp.float32)
            before, after = left_cols[:, row - 1 : row], right_cols[:, row - 1 : row]
        west = jnp.where(lane == 0, before, pltpu.roll(block, 1, 1))
        east = jnp.where(lane == LANES - 1, after, pltpu.roll(block, LANES - 1, 1))
        cells = slice(row * LANES, (row + 1) * LANES)
        x3_ref[:channels, cells] = west.astype(jnp.bfloat16)
        x3_ref[channels : 2 * channels, cells] = block.astype(jnp.bfloat16)
        x3_ref[2 * channels :, cells] = east.astype(jnp.bfloat16)
    for pair in range(rows // 2):
        start = 2 * pair * LANES
        pre = b_ref[...] + jnp.zeros((channels, 2 * LANES), jnp.float32)
        for tap_row in range(3):
            begin = start + tap_row * LANES
            pre = pre + dot(w_ref[tap_row], x3_ref[:, begin : begin + 2 * LANES])
        sigmoid = 1.0 / (1.0 + jnp.exp(-pre))
        active = (pre * sigmoid).astype(jnp.bfloat16)
        slope_ref[:, start : start + 2 * LANES] = sigmoid * (1.0 + pre * (1.0 - sigmoid))
        result = dot(ow_ref[...], active) + ob_ref[...]
        out_ref[:, start : start + 2 * LANES] = result.astype(jnp.bfloat16)


def backward_kernel(rows, shares, members, own_ref, peer_refs, target_ref, vw_ref, owt_ref, slope_ref, x3_ref, wb_ref,
                    grad_ref, right_ref, left_ref, even_ref, odd_ref, g_ref):
    channels = slope_ref.shape[0]
    cells = rows * LANES
    eps = smoothing * smoothing

    def signed(d):
        return d * lax.rsqrt(d * d + eps)

    g_ref[:, : 2 * LANES] = jnp.zeros((channels, 2 * LANES), jnp.bfloat16)
    g_ref[:, 2 * LANES + cells :] = jnp.zeros((channels, 2 * LANES), jnp.bfloat16)
    for pair in range(rows // 2):
        here = slice(2 * pair * LANES, 2 * (pair + 1) * LANES)
        own = own_ref[:, here].astype(jnp.float32)
        total = jnp.zeros_like(own)
        for peer_ref in peer_refs:
            total = total + signed(own - peer_ref[:, here].astype(jnp.float32))
        fit = signed(own - target_ref[:, here])
        grad_out = vw_ref[...] * (fit / members - total / (members * (members - 1)))
        grad_act = dot(owt_ref[...], grad_out.astype(jnp.bfloat16))
        g_ref[:, 2 * LANES + here.start : 2 * LANES + here.stop] = (grad_act * slope_ref[:, here]).astype(jnp.bfloat16)

    grad_pre = g_ref[:, 2 * LANES : 2 * LANES + cells]
    terms = []
    for tap_row in range(3):
        terms.append(dot(x3_ref[:, tap_row * LANES : tap_row * LANES + cells], grad_pre, (((1,), (1,)), ((), ()))))
    size = channels // shares
    for parity, ref in ((0, even_ref), (1, odd_ref)):
        pieces = []
        for share in range(parity, shares, 2):
            for tap in range(9):
                begin = (tap % 3) * channels + share * size
                pieces.append(terms[tap // 3][begin : begin + size])
        ref[...] = jnp.concatenate(pieces, axis=0).astype(jnp.bfloat16)

    lane = lax.broadcasted_iota(jnp.int32, (channels, LANES), 1)
    right = jnp.zeros((channels, LANES), jnp.float32)
    left = jnp.zeros((channels, LANES), jnp.float32)
    for pair in range((rows + 2) // 2):
        start = 2 * pair * LANES
        spread = jnp.zeros((3 * channels, 2 * LANES), jnp.float32)
        for tap_row in range(3):
            begin = start + (2 - tap_row) * LANES
            spread = spread + dot(wb_ref[tap_row], g_ref[:, begin : begin + 2 * LANES])
        for half in range(2):
            row = 2 * pair + half
            part = slice(half * LANES, (half + 1) * LANES)
            to_west = spread[:channels, part]
            to_east = spread[2 * channels :, part]
            moved_west = pltpu.roll(to_west, LANES - 1, 1)
            moved_east = pltpu.roll(to_east, 1, 1)
            total = spread[channels : 2 * channels, part]
            total = total + jnp.where(lane == LANES - 1, 0.0, moved_west) + jnp.where(lane == 0, 0.0, moved_east)
            grad_ref[:, row * LANES : (row + 1) * LANES] = total
            left = jnp.where(lane == row, pltpu.roll(to_west, row, 1) if row else to_west, left)
            right = jnp.where(lane == row, pltpu.roll(to_east, row + 1, 1), right)
    left_ref[...] = left[:, : rows + 2]
    right_ref[...] = right[:, : rows + 2]


def ring_pairs(bands, loops):
    half = loops // 2
    pairs = []
    for band in range(bands):
        for loop in range(loops):
            if loop < half:
                goal = (band + 1, loop) if band + 1 < bands else (band, loop + half)
            else:
                goal = (band - 1, loop) if band > 0 else (band, loop - half)
            pairs.append((band * loops + loop, goal[0] * loops + goal[1]))
    return pairs, [(j, i) for i, j in pairs]


def flipped(size, bit):
    return [(i, i ^ bit) for i in range(size)]


def total_of(value, axis, bits):
    size = lax.axis_size(axis)
    parts = [value]
    for k in range(1, bits):
        parts.append(lax.ppermute(value, axis, flipped(size, k)))
    return parts


def butterfly(values):
    values = [v.astype(jnp.float32) for v in values]
    while len(values) > 1:
        values = [values[i] + values[i + 1] for i in range(0, len(values), 2)]
    return values[0]


def pallas(kernel, out_shape, scratch=(), flops=0, nbytes=0):
    return pl.pallas_call(
        kernel,
        out_shape=out_shape,
        scratch_shapes=list(scratch),
        compiler_params=pltpu.CompilerParams(vmem_limit_bytes=48 * 1024 * 1024),
        cost_estimate=pl.CostEstimate(flops=flops, bytes_accessed=nbytes, transcendentals=0),
    )


def on_device(features, conv_weight, conv_bias, out_weight, out_bias, var_weight, target):
    field = features[0]
    channels, rows, cols = field.shape
    variables = out_weight.shape[0]
    members = lax.axis_size("ens")
    bands, loops = lax.axis_size("lat"), lax.axis_size("lon")
    loop = lax.axis_index("lon")
    cells = rows * cols
    f32, bf16 = jnp.float32, jnp.bfloat16
    east_way = [(i, (i + 1) % loops) for i in range(loops)]
    west_way = [(j, i) for i, j in east_way]
    onward, back = ring_pairs(bands, loops)
    near = loop < loops // 2

    flat = field.reshape(channels, cells)
    left = lax.ppermute(field[:, :, cols - 1], "lon", east_way)
    right = lax.ppermute(field[:, :, 0], "lon", west_way)
    first = jnp.concatenate([field[:, 0], left[:, :1], right[:, :1]], axis=1)
    last = jnp.concatenate([field[:, rows - 1], left[:, rows - 1 :], right[:, rows - 1 :]], axis=1)
    got_on = lax.ppermute(jnp.where(near, last, first), ("lat", "lon"), onward)
    got_back = lax.ppermute(jnp.where(near, first, last), ("lat", "lon"), back)
    north = jnp.where(near, got_on, got_back)
    south = jnp.where(near, got_back, got_on)

    taps = conv_weight.reshape(channels, 3, 3, channels)
    w_forward = taps.transpose(1, 3, 2, 0).reshape(3, channels, 3 * channels)
    w_backward = taps.transpose(1, 2, 0, 3).reshape(3, 3 * channels, channels)
    truth = target.reshape(variables, cells)

    own, slope, x3 = pallas(
        functools.partial(forward_kernel, rows),
        (
            jax.ShapeDtypeStruct((variables, cells), bf16),
            jax.ShapeDtypeStruct((channels, cells), f32),
            jax.ShapeDtypeStruct((3 * channels, cells + 2 * cols), bf16),
        ),
        flops=2 * cells * channels * (9 * channels + variables),
    )(flat, north, south, left, right, w_forward, conv_bias[:, None], out_weight, out_bias[:, None])

    peers = total_of(own, "ens", members)[1:]

    def kernel(own_ref, p1, p2, p3, *rest):
        backward_kernel(rows, loops, members, own_ref, (p1, p2, p3), *rest)

    share_rows = 9 * channels // 2
    grad, rim_right, rim_left, even, odd = pallas(
        kernel,
        (
            jax.ShapeDtypeStruct((channels, cells + 2 * cols), f32),
            jax.ShapeDtypeStruct((channels, rows + 2), f32),
            jax.ShapeDtypeStruct((channels, rows + 2), f32),
            jax.ShapeDtypeStruct((share_rows, channels), bf16),
            jax.ShapeDtypeStruct((share_rows, channels), bf16),
        ),
        scratch=[pltpu.VMEM((channels, cells + 4 * cols), bf16)],
        flops=2 * cells * channels * (18 * channels + variables),
    )(own, *peers, truth, var_weight[:, None], out_weight.T, slope, x3, w_backward)

    is_odd = (loop % 2) == 1
    got = lax.ppermute(jnp.where(is_odd, even, odd), "lon", flipped(loops, 1))
    kept = jnp.where(is_odd, odd, even).astype(f32) + got.astype(f32)
    block = 9 * channels // loops

    from_left = lax.ppermute(rim_right.astype(bf16), "lon", east_way).astype(f32)
    from_right = lax.ppermute(rim_left.astype(bf16), "lon", west_way).astype(f32)
    grad3 = grad.reshape(channels, rows + 2, cols)
    grad3 = grad3 + jnp.pad(from_left[:, :, None], ((0, 0), (0, 0), (0, cols - 1)))
    grad3 = grad3 + jnp.pad(from_right[:, :, None], ((0, 0), (0, 0), (cols - 1, 0)))
    top, bottom = grad3[:, 0].astype(bf16), grad3[:, rows + 1].astype(bf16)
    got_back = lax.ppermute(jnp.where(near, top, bottom), ("lat", "lon"), back)
    got_on = lax.ppermute(jnp.where(near, bottom, top), ("lat", "lon"), onward)
    to_first = jnp.where(near, got_on, got_back).astype(f32)
    to_last = jnp.where(near, got_back, got_on).astype(f32)
    core = grad3[:, 1 : rows + 1]
    core = core + jnp.pad(to_first[:, None], ((0, 0), (0, rows - 1), (0, 0)))
    core = core + jnp.pad(to_last[:, None], ((0, 0), (rows - 1, 0), (0, 0)))
    grad_features = core.astype(bf16)[None]

    bit = loops // 2
    kept = kept.astype(bf16).reshape(loops // 2, block, channels)
    while bit > 1:
        mine = (loop // bit) % 2
        half = kept.shape[0] // 2
        send = jnp.where(mine == 1, kept[:half], kept[half:])
        hold = jnp.where(mine == 1, kept[half:], kept[:half])
        got = lax.ppermute(send, "lon", flipped(loops, bit))
        kept = (hold.astype(f32) + got.astype(f32)).astype(bf16)
        bit //= 2
    share = kept[0]
    share = butterfly(total_of(share, "ens", members)).astype(bf16)
    bit = 1
    while bit < bands:
        share = butterfly([share, lax.ppermute(share, "lat", flipped(bands, bit))]).astype(bf16 if 2 * bit < bands else f32)
        bit *= 2
    total_cells = members * cells * bands * loops
    grad_weight = (share / math.sqrt(total_cells)).reshape(9, channels // loops, channels).transpose(1, 0, 2)
    return grad_features, grad_weight


def solution(mesh):
    return jax.shard_map(
        on_device,
        mesh=mesh,
        in_specs=(P("ens", None, "lat", "lon"), P(), P(), P(), P(), P(), P(None, "lat", "lon")),
        out_specs=(P("ens", None, "lat", "lon"), P("lon", None, None)),
        check_vma=False,
    )
```

```python
import functools
import math

import jax
import jax.numpy as jnp
from jax import lax
from jax.experimental import pallas as pl
from jax.experimental.pallas import tpu as pltpu
from jax.sharding import PartitionSpec as P

smoothing = 0.1
LANES = 128


def dot(a, b, dims=(((1,), (0,)), ((), ()))):
    return lax.dot_general(a, b, dims, preferred_element_type=jnp.float32)


def prepare_kernel(x_ref, flat_ref, east_ref, west_ref, wide_ref):
    channels, rows, cols = wide_ref.shape
    wide_ref[...] = x_ref[0].astype(jnp.float32)
    for row in range(rows):
        flat_ref[:, row * cols : (row + 1) * cols] = wide_ref[:, row, :].astype(jnp.bfloat16)
    cell = lax.broadcasted_iota(jnp.int32, (rows * cols, 2 * rows), 0)
    slot = lax.broadcasted_iota(jnp.int32, (rows * cols, 2 * rows), 1)
    wanted = jnp.where(slot < rows, slot * cols + (cols - 1), (slot - rows) * cols)
    pick = jnp.where(cell == wanted, 1.0, 0.0).astype(jnp.bfloat16)
    edges = dot(flat_ref[...], pick).astype(jnp.bfloat16)
    east_ref[...] = edges[:, :rows]
    west_ref[...] = edges[:, rows:]


def forward_kernel(rows, x_ref, north_ref, south_ref, left_ref, right_ref, w_ref, b_ref, ow_ref, ob_ref,
                   out_ref, slope_ref, x3_ref):
    channels = x_ref.shape[0]
    lane = lax.broadcasted_iota(jnp.int32, (channels, LANES), 1)
    left_cols = left_ref[...].astype(jnp.float32)
    right_cols = right_ref[...].astype(jnp.float32)
    north = north_ref[...].astype(jnp.float32)
    south = south_ref[...].astype(jnp.float32)
    weights = w_ref[...].T
    for row in range(rows + 2):
        if row == 0:
            block, before, after = north[:, :LANES], north[:, LANES : LANES + 1], north[:, LANES + 1 :]
        elif row == rows + 1:
            block, before, after = south[:, :LANES], south[:, LANES : LANES + 1], south[:, LANES + 1 :]
        else:
            block = x_ref[:, (row - 1) * LANES : row * LANES].astype(jnp.float32)
            before, after = left_cols[:, row - 1 : row], right_cols[:, row - 1 : row]
        west = jnp.where(lane == 0, before, pltpu.roll(block, 1, 1))
        east = jnp.where(lane == LANES - 1, after, pltpu.roll(block, LANES - 1, 1))
        cells = slice(row * LANES, (row + 1) * LANES)
        x3_ref[:channels, cells] = west.astype(jnp.bfloat16)
        x3_ref[channels : 2 * channels, cells] = block.astype(jnp.bfloat16)
        x3_ref[2 * channels :, cells] = east.astype(jnp.bfloat16)
    for pair in range(rows // 2):
        start = 2 * pair * LANES
        pre = b_ref[...] + jnp.zeros((channels, 2 * LANES), jnp.float32)
        for tap_row in range(3):
            begin = start + tap_row * LANES
            taps = weights[:, tap_row * 3 * channels : (tap_row + 1) * 3 * channels]
            pre = pre + dot(taps, x3_ref[:, begin : begin + 2 * LANES])
        sigmoid = 1.0 / (1.0 + jnp.exp(-pre))
        active = (pre * sigmoid).astype(jnp.bfloat16)
        slope_ref[:, start : start + 2 * LANES] = sigmoid * (1.0 + pre * (1.0 - sigmoid))
        result = dot(ow_ref[...], active) + ob_ref[...]
        out_ref[:, start : start + 2 * LANES] = result.astype(jnp.bfloat16)


def backward_kernel(rows, shares, members, own_ref, all_ref, target_ref, vw_ref, owt_ref, slope_ref, x3_ref, w_ref,
                    core_ref, rims_ref, right_ref, left_ref, term_ref, g_ref):
    channels = slope_ref.shape[0]
    cells = rows * LANES
    eps = smoothing * smoothing

    def signed(d):
        return d * lax.rsqrt(d * d + eps)

    g_ref[:, : 2 * LANES] = jnp.zeros((channels, 2 * LANES), jnp.bfloat16)
    g_ref[:, 2 * LANES + cells :] = jnp.zeros((channels, 2 * LANES), jnp.bfloat16)
    for pair in range(rows // 2):
        here = slice(2 * pair * LANES, 2 * (pair + 1) * LANES)
        own = own_ref[:, here].astype(jnp.float32)
        total = jnp.zeros_like(own)
        for member in range(members):
            total = total + signed(own - all_ref[member, :, here].astype(jnp.float32))
        truth = jnp.concatenate([target_ref[:, 2 * pair, :], target_ref[:, 2 * pair + 1, :]], axis=1)
        fit = signed(own - truth)
        grad_out = vw_ref[...] * (fit / members - total / (members * (members - 1)))
        grad_act = dot(owt_ref[...], grad_out.astype(jnp.bfloat16))
        g_ref[:, 2 * LANES + here.start : 2 * LANES + here.stop] = (grad_act * slope_ref[:, here]).astype(jnp.bfloat16)

    grad_pre = g_ref[:, 2 * LANES : 2 * LANES + cells]
    terms = []
    for tap_row in range(3):
        terms.append(dot(x3_ref[:, tap_row * LANES : tap_row * LANES + cells], grad_pre, (((1,), (1,)), ((), ()))))
    size = channels // shares
    pieces = []
    for loop_half in range(2):
        for taps in (range(5), range(5, 10)):
            for share in range(loop_half * shares // 2, (loop_half + 1) * shares // 2):
                for tap in taps:
                    if tap < 9:
                        begin = (tap % 3) * channels + share * size
                        pieces.append(terms[tap // 3][begin : begin + size])
                    else:
                        pieces.append(jnp.zeros((size, channels), jnp.float32))
    term_ref[...] = jnp.concatenate(pieces, axis=0).astype(jnp.bfloat16)

    lane = lax.broadcasted_iota(jnp.int32, (channels, LANES), 1)
    right = jnp.zeros((channels, LANES), jnp.float32)
    left = jnp.zeros((channels, LANES), jnp.float32)
    for pair in range((rows + 2) // 2):
        start = 2 * pair * LANES
        spread = jnp.zeros((3 * channels, 2 * LANES), jnp.float32)
        for tap_row in range(3):
            begin = start + (2 - tap_row) * LANES
            taps = w_ref[tap_row * 3 * channels : (tap_row + 1) * 3 * channels, :]
            spread = spread + dot(taps, g_ref[:, begin : begin + 2 * LANES])
        for half in range(2):
            row = 2 * pair + half
            part = slice(half * LANES, (half + 1) * LANES)
            to_west = spread[:channels, part]
            to_east = spread[2 * channels :, part]
            moved_west = pltpu.roll(to_west, LANES - 1, 1)
            moved_east = pltpu.roll(to_east, 1, 1)
            total = spread[channels : 2 * channels, part]
            total = total + jnp.where(lane == LANES - 1, 0.0, moved_west) + jnp.where(lane == 0, 0.0, moved_east)
            if row == 0:
                rims_ref[:, :LANES] = total
            elif row == rows + 1:
                rims_ref[:, LANES:] = total
            else:
                core_ref[:, (row - 1) * LANES : row * LANES] = total
            left = jnp.where(lane == row, pltpu.roll(to_west, row, 1) if row else to_west, left)
            right = jnp.where(lane == row, pltpu.roll(to_east, row + 1, 1), right)
    left_ref[...] = left[:, : rows + 2].astype(jnp.bfloat16)
    right_ref[...] = right[:, : rows + 2].astype(jnp.bfloat16)


def finish_kernel(core_ref, left_ref, right_ref, first_ref, last_ref, out_ref, wide_ref):
    channels, rows, cols = wide_ref.shape
    lane = lax.broadcasted_iota(jnp.int32, (channels, cols), 1)
    left_cols = left_ref[...].astype(jnp.float32)
    right_cols = right_ref[...].astype(jnp.float32)
    for row in range(rows):
        total = core_ref[:, row * cols : (row + 1) * cols]
        total = total + jnp.where(lane == 0, left_cols[:, row + 1 : row + 2], 0.0)
        total = total + jnp.where(lane == cols - 1, right_cols[:, row + 1 : row + 2], 0.0)
        if row == 0:
            total = total + first_ref[...].astype(jnp.float32)
        if row == rows - 1:
            total = total + last_ref[...].astype(jnp.float32)
        wide_ref[:, row, :] = total
    out_ref[0] = wide_ref[...].astype(jnp.bfloat16)


def ring_pairs(bands, loops):
    half = loops // 2
    pairs = []
    for band in range(bands):
        for loop in range(loops):
            if loop < half:
                goal = (band + 1, loop) if band + 1 < bands else (band, loop + half)
            else:
                goal = (band - 1, loop) if band > 0 else (band, loop - half)
            pairs.append((band * loops + loop, goal[0] * loops + goal[1]))
    return pairs, [(j, i) for i, j in pairs]


def exchange(pieces, groups):
    return lax.all_to_all(
        pieces, ("ens", "lat", "lon"), split_axis=0, concat_axis=0, axis_index_groups=groups, tiled=True
    )


def pallas(kernel, out_shape, scratch=(), flops=0, nbytes=0):
    return pl.pallas_call(
        kernel,
        out_shape=out_shape,
        scratch_shapes=list(scratch),
        compiler_params=pltpu.CompilerParams(vmem_limit_bytes=48 * 1024 * 1024),
        cost_estimate=pl.CostEstimate(flops=flops, bytes_accessed=nbytes, transcendentals=0),
    )


def on_device(features, conv_weight, conv_bias, out_weight, out_bias, var_weight, target):
    channels, rows, cols = features.shape[1:]
    variables = out_weight.shape[0]
    members = lax.axis_size("ens")
    bands, loops = lax.axis_size("lat"), lax.axis_size("lon")
    half = loops // 2
    loop = lax.axis_index("lon")
    cells = rows * cols
    f32, bf16 = jnp.float32, jnp.bfloat16
    shape = jax.ShapeDtypeStruct
    east_way = [(i, (i + 1) % loops) for i in range(loops)]
    west_way = [(j, i) for i, j in east_way]
    onward, back = ring_pairs(bands, loops)
    near = loop < half

    def place(member, band, spot):
        return (member * bands + band) * loops + spot

    level_groups = [
        [place(e, b, h * half + s) for e in range(members) for s in range(half)] for b in range(bands) for h in range(2)
    ]
    column_groups = [
        [place(e, b, h * half + s) for h in range(2) for b in range(bands)] for e in range(members) for s in range(half)
    ]
    member_groups = [[place(e, b, s) for e in range(members)] for b in range(bands) for s in range(loops)]

    flat, east, west = pallas(
        prepare_kernel,
        (shape((channels, cells), bf16), shape((channels, rows), bf16), shape((channels, rows), bf16)),
        scratch=[pltpu.VMEM((channels, rows, cols), f32)],
    )(features)
    left = lax.ppermute(east, "lon", east_way)
    right = lax.ppermute(west, "lon", west_way)
    first = jnp.concatenate([flat[:, :cols], left[:, :1], right[:, :1]], axis=1)
    last = jnp.concatenate([flat[:, cells - cols :], left[:, rows - 1 :], right[:, rows - 1 :]], axis=1)
    got_on = lax.ppermute(jnp.where(near, last, first), ("lat", "lon"), onward)
    got_back = lax.ppermute(jnp.where(near, first, last), ("lat", "lon"), back)
    north = jnp.where(near, got_on, got_back)
    south = jnp.where(near, got_back, got_on)

    weights = conv_weight.transpose(1, 0, 2).reshape(9 * channels, channels)

    own, slope, x3 = pallas(
        functools.partial(forward_kernel, rows),
        (
            shape((variables, cells), bf16),
            shape((channels, cells), f32),
            shape((3 * channels, cells + 2 * cols), bf16),
        ),
        flops=2 * cells * channels * (9 * channels + variables),
    )(flat, north, south, left, right, weights, conv_bias[:, None], out_weight, out_bias[:, None])

    everyone = exchange(jnp.broadcast_to(own, (members, variables, cells)), member_groups)

    core, rims, rim_right, rim_left, terms = pallas(
        functools.partial(backward_kernel, rows, loops, members),
        (
            shape((channels, cells), f32),
            shape((channels, 2 * cols), f32),
            shape((channels, rows + 2), bf16),
            shape((channels, rows + 2), bf16),
            shape((10 * channels, channels), bf16),
        ),
        scratch=[pltpu.VMEM((channels, cells + 4 * cols), bf16)],
        flops=2 * cells * channels * (18 * channels + variables),
    )(own, everyone, target, var_weight[:, None], out_weight.T, slope, x3, weights)

    from_left = lax.ppermute(rim_right, "lon", east_way)
    from_right = lax.ppermute(rim_left, "lon", west_way)

    size = 5 * channels // loops
    terms = exchange(terms.reshape(members * half, size, channels), level_groups)
    terms = jnp.sum(terms.astype(f32), axis=0).astype(bf16)

    lane = lax.broadcasted_iota(jnp.int32, (channels, cols), 1)
    wide = [
        jnp.where(lane == 0, from_left[:, r : r + 1].astype(f32), 0.0)
        + jnp.where(lane == cols - 1, from_right[:, r : r + 1].astype(f32), 0.0)
        for r in (0, rows + 1)
    ]
    top = (rims[:, :cols] + wide[0]).astype(bf16)
    bottom = (rims[:, cols:] + wide[1]).astype(bf16)
    got_back = lax.ppermute(jnp.where(near, top, bottom), ("lat", "lon"), back)
    got_on = lax.ppermute(jnp.where(near, bottom, top), ("lat", "lon"), onward)
    to_first = jnp.where(near, got_on, got_back)
    to_last = jnp.where(near, got_back, got_on)

    terms = exchange(jnp.broadcast_to(terms, (2 * bands, size, channels)), column_groups)
    terms = jnp.sum(terms.astype(f32), axis=0).astype(bf16)

    grad_features = pallas(
        finish_kernel,
        shape((1, channels, rows, cols), bf16),
        scratch=[pltpu.VMEM((channels, rows, cols), f32)],
    )(core, from_left, from_right, to_first, to_last)

    terms = exchange(jnp.broadcast_to(terms, (members, size, channels)), member_groups)
    share = jnp.where(near, terms[: members // 2], terms[members // 2 :]).reshape(2 * size, channels)
    share = share[: 9 * channels // loops].astype(f32)
    total_cells = members * cells * bands * loops
    grad_weight = (share / math.sqrt(total_cells)).reshape(9, channels // loops, channels).transpose(1, 0, 2)
    return grad_features, grad_weight


def solution(mesh):
    return jax.shard_map(
        on_device,
        mesh=mesh,
        in_specs=(P("ens", None, "lat", "lon"), P(), P(), P(), P(), P(), P(None, "lat", "lon")),
        out_specs=(P("ens", None, "lat", "lon"), P("lon", None, None)),
        check_vma=False,
    )
```

```python
import functools
import math

import jax
import jax.numpy as jnp
import numpy as np
from jax import lax
from jax.experimental import pallas as pl
from jax.experimental.pallas import tpu as pltpu
from jax.sharding import PartitionSpec as P

smoothing = 0.1
LANES = 128
RIM = 32
f32, bf16 = jnp.float32, jnp.bfloat16


def dot(a, b, dims=(((1,), (0,)), ((), ()))):
    return lax.dot_general(a, b, dims, preferred_element_type=f32)


def tile(index, count=1):
    return slice(index * LANES, (index + count) * LANES)


def signed(d):
    return d * lax.rsqrt(d * d + smoothing * smoothing)


def prepare_kernel(x_ref, target_ref, flat_ref, east_ref, west_ref, first_ref, last_ref, wide_ref, aim_ref):
    channels, rows, cols = wide_ref.shape
    variables = target_ref.shape[0]
    wide_ref[...] = x_ref[0].astype(f32)
    aim_ref[...] = jnp.zeros(aim_ref.shape, f32)
    for row in range(rows):
        flat_ref[:, tile(row)] = wide_ref[:, row, :].astype(bf16)
        aim_ref[:variables, tile(row)] = target_ref[:, row, :]
    high = aim_ref[...].astype(bf16)
    low = (aim_ref[...] - high.astype(f32)).astype(bf16)
    cell = lax.broadcasted_iota(jnp.int32, (rows * cols, 4 * rows), 0)
    slot = lax.broadcasted_iota(jnp.int32, (rows * cols, 4 * rows), 1)
    column = jnp.where(slot < rows, cols - 1, jnp.where(slot < 2 * rows, cols - 2, jnp.where(slot < 3 * rows, 0, 1)))
    wanted = (slot % rows) * cols + column
    pick = jnp.where(cell == wanted, 1.0, 0.0).astype(bf16)
    edges = dot(flat_ref[...], pick).astype(bf16)
    high_edges = dot(high, pick).astype(bf16)
    low_edges = dot(low, pick).astype(bf16)
    for ref, begin in ((east_ref, 0), (west_ref, 2 * rows)):
        ref[:channels] = edges[:, begin : begin + 2 * rows]
        ref[channels:, :rows] = high_edges[:, begin : begin + rows]
        ref[channels:, rows:] = low_edges[:, begin : begin + rows]
    for ref, near, second in ((first_ref, 0, 1), (last_ref, rows - 1, rows - 2)):
        ref[:channels, :cols] = flat_ref[:, tile(near)]
        ref[:channels, cols:] = flat_ref[:, tile(second)]
        ref[channels:, :cols] = high[:, tile(near)]
        ref[channels:, cols:] = low[:, tile(near)]


def rim_choice(rows):
    width = 2 * LANES + 8
    sources = [np.zeros((size, 3 * LANES), np.float32) for size in (2 * rows, 2 * rows, 2 * rows, 2 * rows, width, width)]
    left, right, east, west, north, south = sources
    for row in range(rows):
        lane = row + 2
        left[row, LANES + lane] = 1
        left[rows + row, lane] = 1
        right[row, LANES + RIM + lane] = 1
        right[rows + row, 2 * LANES + RIM + lane] = 1
        east[row, RIM + lane] = 1
        west[row, 2 * LANES + lane] = 1
    for source, lanes in ((north, (1, 0)), (south, (rows + 2, rows + 3))):
        for second, lane in enumerate(lanes):
            source[2 * LANES + second, LANES + lane] = 1
            source[2 * LANES + 2 + second, lane] = 1
            source[2 * LANES + 4 + second, LANES + RIM + lane] = 1
            source[2 * LANES + 6 + second, 2 * LANES + RIM + lane] = 1
            source[second * LANES + LANES - 1, RIM + lane] = 1
            source[second * LANES, 2 * LANES + lane] = 1
    return [jnp.asarray(source, bf16) for source in sources]


def forward_kernel(rows, pole_ref, x_ref, north_ref, south_ref, left_ref, right_ref, east_ref, west_ref,
                   cl_ref, cr_ref, ce_ref, cw_ref, cn_ref, cs_ref, w_ref, b_ref, ow_ref, ob_ref,
                   out_ref, slope_ref, x3_ref, truth_ref):
    channels = x_ref.shape[0]
    variables = out_ref.shape[0]
    north_pole, south_pole = pole_ref[0], pole_ref[1]
    lane = lax.broadcasted_iota(jnp.int32, (channels, LANES), 1)
    lane3 = lax.broadcasted_iota(jnp.int32, (3 * channels, LANES), 1)
    left = left_ref[:channels].astype(f32)
    right = right_ref[:channels].astype(f32)
    north = north_ref[:channels].astype(f32)
    south = south_ref[:channels].astype(f32)
    weights = w_ref[...].T

    def taps(tap_row):
        return weights[:, tap_row * 3 * channels : (tap_row + 1) * 3 * channels]

    for row in range(rows + 4):
        if row < 2 or row >= rows + 2:
            edge = north if row < 2 else south
            second = 1 - row if row < 2 else row - rows - 2
            block = edge[:, tile(second)]
            before = edge[:, 2 * LANES + second : 2 * LANES + second + 1]
            after = edge[:, 2 * LANES + 4 + second : 2 * LANES + 5 + second]
        else:
            block = x_ref[:, tile(row - 2)].astype(f32)
            before, after = left[:, row - 2 : row - 1], right[:, row - 2 : row - 1]
        x3_ref[:channels, tile(row)] = jnp.where(lane == 0, before, pltpu.roll(block, 1, 1)).astype(bf16)
        x3_ref[channels : 2 * channels, tile(row)] = block.astype(bf16)
        x3_ref[2 * channels :, tile(row)] = jnp.where(
            lane == LANES - 1, after, pltpu.roll(block, LANES - 1, 1)
        ).astype(bf16)

    def finish(pre, place):
        pre = pre + b_ref[...]
        sigmoid = 1.0 / (1.0 + jnp.exp(-pre))
        active = (pre * sigmoid).astype(bf16)
        slope_ref[:, place] = sigmoid * (1.0 + pre * (1.0 - sigmoid))
        out_ref[:, place] = (dot(ow_ref[...], active) + ob_ref[...]).astype(bf16)

    for pair in range(rows // 2):
        begin = 1 + 2 * pair
        pre = dot(taps(0), x3_ref[:, tile(begin, 2)])
        for tap_row in (1, 2):
            pre = pre + dot(taps(tap_row), x3_ref[:, tile(begin + tap_row, 2)])
        finish(pre, tile(begin, 2))
    for q, pole in ((0, north_pole), (rows + 1, south_pole)):
        above, below = x3_ref[:, tile(q)].astype(f32), x3_ref[:, tile(q + 2)].astype(f32)
        turned = lane3 < pole * LANES
        pre = dot(taps(1), x3_ref[:, tile(q + 1)])
        pre = pre + dot(taps(0), jnp.where(turned, below, above).astype(bf16))
        pre = pre + dot(taps(2), jnp.where(turned, above, below).astype(bf16))
        finish(pre, tile(q))
    rim = dot(left_ref[...], cl_ref[...]) + dot(right_ref[...], cr_ref[...])
    rim = rim + dot(east_ref[...], ce_ref[...]) + dot(west_ref[...], cw_ref[...])
    rim = rim + dot(north_ref[...], cn_ref[...]) + dot(south_ref[...], cs_ref[...])
    middle = jnp.concatenate([rim[:channels, tile(k)] for k in range(3)], axis=0)
    above, below = pltpu.roll(middle, 1, 1), pltpu.roll(middle, LANES - 1, 1)
    first = (lane3 == 1) | (lane3 == RIM + 1)
    last = (lane3 == rows + 2) | (lane3 == RIM + rows + 2)
    turned = (first & (lane3 < north_pole * LANES)) | (last & (lane3 < south_pole * LANES))
    pre = dot(taps(1), middle.astype(bf16))
    pre = pre + dot(taps(0), jnp.where(turned, below, above).astype(bf16))
    pre = pre + dot(taps(2), jnp.where(turned, above, below).astype(bf16))
    finish(pre, tile(rows + 2))
    aim = slice(channels, channels + variables)
    for place, ref in ((0, north_ref), (1, south_ref)):
        edge = ref[channels:, tile(0)].astype(f32) + ref[channels:, tile(1)].astype(f32)
        truth_ref[:, tile(place)] = edge[:variables]
    side = lax.broadcasted_iota(jnp.int32, (variables, LANES), 1)
    truth_ref[:, tile(2)] = rim[aim, tile(1)] + jnp.where(side < RIM, rim[aim, tile(0)], rim[aim, tile(2)])


def weight_kernel(rows, shares, members, own_ref, all_ref, target_ref, truth_ref, vw_ref, owt_ref, slope_ref, x3_ref,
                  g_ref, term_ref):
    channels = slope_ref.shape[0]

    def grad(place, truth):
        own = own_ref[:, place].astype(f32)
        total = jnp.zeros_like(own)
        for member in range(members):
            total = total + signed(own - all_ref[member, :, place].astype(f32))
        grad_out = vw_ref[...] * (signed(own - truth) / members - total / (members * (members - 1)))
        grad_act = dot(owt_ref[...], grad_out.astype(bf16))
        g_ref[:, place] = (grad_act * slope_ref[:, place]).astype(bf16)

    for pair in range(rows // 2):
        truth = jnp.concatenate([target_ref[:, 2 * pair, :], target_ref[:, 2 * pair + 1, :]], axis=1)
        grad(tile(1 + 2 * pair, 2), truth)
    for place, q in enumerate((0, rows + 1, rows + 2)):
        grad(tile(q), truth_ref[:, tile(place)])

    grad_pre = g_ref[:, tile(1, rows)]
    terms = []
    for tap_row in range(3):
        terms.append(dot(x3_ref[:, tile(1 + tap_row, rows)], grad_pre, (((1,), (1,)), ((), ()))))
    size = channels // shares
    pieces = []
    for loop_half in range(2):
        for taps in (range(5), range(5, 10)):
            for share in range(loop_half * shares // 2, (loop_half + 1) * shares // 2):
                for tap in taps:
                    if tap < 9:
                        begin = (tap % 3) * channels + share * size
                        pieces.append(terms[tap // 3][begin : begin + size])
                    else:
                        pieces.append(jnp.zeros((size, channels), f32))
    term_ref[...] = jnp.concatenate(pieces, axis=0).astype(bf16)


def feature_kernel(pole_ref, g_ref, w_ref, out_ref, wide_ref):
    channels, rows, cols = wide_ref.shape
    north_pole, south_pole = pole_ref[0], pole_ref[1]
    lane = lax.broadcasted_iota(jnp.int32, (channels, LANES), 1)

    def taps(tap_row):
        return w_ref[tap_row * 3 * channels : (tap_row + 1) * 3 * channels, :]

    def split(value, turned):
        kept = jnp.where(turned, 0.0, value)
        return kept.astype(bf16), (value - kept).astype(bf16)

    north, north_turned = split(g_ref[:, tile(0)].astype(f32), lane < north_pole * LANES)
    south, south_turned = split(g_ref[:, tile(rows + 1)].astype(f32), lane < south_pole * LANES)
    rim = g_ref[:, tile(rows + 2)].astype(f32)
    above, below = pltpu.roll(rim, 1, 1), pltpu.roll(rim, LANES - 1, 1)
    first = (lane == 2) | (lane == RIM + 2)
    last = (lane == rows + 1) | (lane == RIM + rows + 1)
    above, above_turned = split(above, first & (lane < north_pole * LANES))
    below, below_turned = split(below, last & (lane < south_pole * LANES))
    side = dot(taps(1), rim.astype(bf16))
    side = side + dot(taps(2), above) + dot(taps(0), below)
    side = side + dot(taps(0), above_turned) + dot(taps(2), below_turned)
    from_left, from_right = side[2 * channels :], side[:channels]

    for pair in range(rows // 2):
        row = 2 * pair
        upper = g_ref[:, tile(row, 2)]
        lower = g_ref[:, tile(row + 2, 2)]
        if pair == 0:
            upper = jnp.concatenate([north, g_ref[:, tile(1)]], axis=1)
        if pair == rows // 2 - 1:
            lower = jnp.concatenate([g_ref[:, tile(rows)], south], axis=1)
        spread = dot(taps(1), g_ref[:, tile(row + 1, 2)]) + dot(taps(2), upper) + dot(taps(0), lower)
        for part in range(2):
            block = spread[:, tile(part)]
            if row + part == 0:
                block = block + dot(taps(0), north_turned)
            if row + part == rows - 1:
                block = block + dot(taps(2), south_turned)
            spot = row + part + 2
            moved_west = pltpu.roll(block[:channels], LANES - 1, 1)
            moved_east = pltpu.roll(block[2 * channels :], 1, 1)
            total = block[channels : 2 * channels]
            total = total + jnp.where(lane == 0, from_left[:, spot : spot + 1], moved_east)
            total = total + jnp.where(lane == LANES - 1, from_right[:, RIM + spot : RIM + spot + 1], moved_west)
            wide_ref[:, row + part, :] = total
    out_ref[0] = wide_ref[...].astype(bf16)


def ring_pairs(bands, loops):
    half = loops // 2
    pairs = []
    for band in range(bands):
        for loop in range(loops):
            if loop < half:
                goal = (band + 1, loop) if band + 1 < bands else (band, loop + half)
            else:
                goal = (band - 1, loop) if band > 0 else (band, loop - half)
            pairs.append((band * loops + loop, goal[0] * loops + goal[1]))
    return pairs, [(j, i) for i, j in pairs]


def exchange(pieces, groups):
    return lax.all_to_all(
        pieces, ("ens", "lat", "lon"), split_axis=0, concat_axis=0, axis_index_groups=groups, tiled=True
    )


def pallas(kernel, out_shape, scratch=(), scalars=0, operands=0, flops=0, nbytes=0):
    specs = {}
    if scalars:
        vmem = pl.BlockSpec(memory_space=pltpu.VMEM)
        specs["in_specs"] = [pl.BlockSpec(memory_space=pltpu.SMEM)] + [vmem] * operands
    return pl.pallas_call(
        kernel,
        out_shape=out_shape,
        scratch_shapes=list(scratch),
        compiler_params=pltpu.CompilerParams(vmem_limit_bytes=20 * 1024 * 1024),
        cost_estimate=pl.CostEstimate(flops=flops, bytes_accessed=nbytes, transcendentals=0),
        **specs,
    )


def on_device(features, conv_weight, conv_bias, out_weight, out_bias, var_weight, target):
    channels, rows, cols = features.shape[1:]
    variables = out_weight.shape[0]
    members = lax.axis_size("ens")
    bands, loops = lax.axis_size("lat"), lax.axis_size("lon")
    half = loops // 2
    band, loop = lax.axis_index("lat"), lax.axis_index("lon")
    cells = rows * cols
    more = cells + 3 * cols
    halo = -(-(channels + variables) // 16) * 16
    shape = jax.ShapeDtypeStruct
    east_way = [(i, (i + 1) % loops) for i in range(loops)]
    west_way = [(j, i) for i, j in east_way]
    onward, back = ring_pairs(bands, loops)
    near = loop < half
    poles = jnp.stack([band == 0, band == bands - 1]).astype(jnp.int32)

    def place(member, band, spot):
        return (member * bands + band) * loops + spot

    level_groups = [
        [place(e, b, h * half + s) for e in range(members) for s in range(half)] for b in range(bands) for h in range(2)
    ]
    column_groups = [
        [place(e, b, h * half + s) for h in range(2) for b in range(bands)] for e in range(members) for s in range(half)
    ]
    member_groups = [[place(e, b, s) for e in range(members)] for b in range(bands) for s in range(loops)]

    flat, east, west, first, last = pallas(
        prepare_kernel,
        (
            shape((channels, cells), bf16),
            shape((halo, 2 * rows), bf16),
            shape((halo, 2 * rows), bf16),
            shape((halo, 2 * cols), bf16),
            shape((halo, 2 * cols), bf16),
        ),
        scratch=[pltpu.VMEM((channels, rows, cols), f32), pltpu.VMEM((halo - channels, cells), f32)],
    )(features, target)
    left = lax.ppermute(east, "lon", east_way)
    right = lax.ppermute(west, "lon", west_way)

    def with_corners(edge, near, second):
        picks = [side[:, k : k + 1] for side in (left, right) for k in (near, second, rows + near, rows + second)]
        return jnp.concatenate([edge] + picks, axis=1)

    first = with_corners(first, 0, 1)
    last = with_corners(last, rows - 1, rows - 2)
    got_on = lax.ppermute(jnp.where(near, last, first), ("lat", "lon"), onward)
    got_back = lax.ppermute(jnp.where(near, first, last), ("lat", "lon"), back)
    north = jnp.where(near, got_on, got_back)
    south = jnp.where(near, got_back, got_on)

    weights = conv_weight.transpose(1, 0, 2).reshape(9 * channels, channels)

    own, slope, x3, truth = pallas(
        functools.partial(forward_kernel, rows),
        (
            shape((variables, more), bf16),
            shape((channels, more), f32),
            shape((3 * channels, cells + 4 * cols), bf16),
            shape((variables, 3 * cols), f32),
        ),
        scalars=1,
        operands=17,
        flops=2 * cells * channels * (9 * channels + variables),
    )(
        poles, flat, north, south, left, right, east, west, *rim_choice(rows),
        weights, conv_bias[:, None], out_weight, out_bias[:, None],
    )

    everyone = exchange(jnp.broadcast_to(own, (members, variables, more)), member_groups)

    grads, terms = pallas(
        functools.partial(weight_kernel, rows, loops, members),
        (shape((channels, more), bf16), shape((10 * channels, channels), bf16)),
        flops=2 * cells * channels * (9 * channels + variables),
    )(own, everyone, target, truth, var_weight[:, None], out_weight.T, slope, x3)

    size = 5 * channels // loops
    terms = exchange(terms.reshape(members * half, size, channels), level_groups)
    terms = jnp.sum(terms.astype(f32), axis=0).astype(bf16)

    grad_features = pallas(
        feature_kernel,
        shape((1, channels, rows, cols), bf16),
        scratch=[pltpu.VMEM((channels, rows, cols), f32)],
        scalars=1,
        operands=2,
        flops=2 * cells * channels * 9 * channels,
    )(poles, grads, weights)

    terms = exchange(jnp.broadcast_to(terms, (2 * bands, size, channels)), column_groups)
    terms = jnp.sum(terms.astype(f32), axis=0).astype(bf16)
    terms = exchange(jnp.broadcast_to(terms, (members, size, channels)), member_groups)
    share = jnp.where(near, terms[: members // 2], terms[members // 2 :]).reshape(2 * size, channels)
    share = share[: 9 * channels // loops].astype(f32)
    total_cells = members * cells * bands * loops
    grad_weight = (share / math.sqrt(total_cells)).reshape(9, channels // loops, channels).transpose(1, 0, 2)
    return grad_features, grad_weight


def solution(mesh):
    return jax.shard_map(
        on_device,
        mesh=mesh,
        in_specs=(P("ens", None, "lat", "lon"), P(), P(), P(), P(), P(), P(None, "lat", "lon")),
        out_specs=(P("ens", None, "lat", "lon"), P("lon", None, None)),
        check_vma=False,
    )
```

```python
import functools
import math

import jax
import jax.numpy as jnp
import numpy as np
from jax import lax
from jax.experimental import pallas as pl
from jax.experimental.pallas import tpu as pltpu
from jax.sharding import PartitionSpec as P

smoothing = 0.1
LANES = 128
TAP_QUARTERS = ((0, 1, 2), (3, 4), (5, 6), (7, 8))
VMEM_BYTES = 60 * 2**20
HALO_LANES = 2 * LANES + 16
RIM = 32
f32, bf16 = jnp.float32, jnp.bfloat16


def dot(a, b, dims=(((1,), (0,)), ((), ()))):
    return lax.dot_general(a, b, dims, preferred_element_type=f32)


def tile(index, count=1):
    return slice(index * LANES, (index + count) * LANES)


def signed(d):
    return d * lax.rsqrt(d * d + smoothing * smoothing)


class Copies:
    def __init__(self, sems):
        self.sems, self.made = sems, []

    def start(self, source, goal):
        copy = pltpu.make_async_copy(source, goal, self.sems.at[len(self.made)])
        copy.start()
        self.made.append(copy)
        return copy


def prepare_kernel(odd_ref, x_hbm, target_hbm, flat_hbm, close_hbm, other_hbm, east_hbm, west_hbm, first_hbm, last_hbm,
                   x_ref, target_ref, wide_ref, aim_ref, flat_ref, close_ref, other_ref, east_ref, west_ref, first_ref,
                   last_ref, sems):
    channels, rows, cols = wide_ref.shape
    variables = target_ref.shape[0]
    copies = Copies(sems)
    part = channels // 2
    halves = [slice(k * part, (k + 1) * part) for k in range(2)]
    loads = [copies.start(x_hbm.at[0, here], x_ref.at[here]) for here in halves]
    load_target = copies.start(target_hbm, target_ref)
    cell = lax.broadcasted_iota(jnp.int32, (rows * cols, 4 * rows), 0)
    slot = lax.broadcasted_iota(jnp.int32, (1, 4 * rows), 1)
    column = jnp.where(slot < rows, cols - 1, jnp.where(slot < 2 * rows, cols - 2, jnp.where(slot < 3 * rows, 0, 1)))
    pick = jnp.where(cell == (slot % rows) * cols + column, 1.0, 0.0).astype(bf16)
    aim_ref[variables - variables % 8 :] = jnp.zeros((aim_ref.shape[0] - variables + variables % 8, rows * cols), f32)
    for load, here in zip(loads, halves):
        load.wait()
        wide_ref[here] = x_ref[here].astype(f32)
        for row in range(rows):
            flat_ref[here, tile(row)] = wide_ref[here, row, :].astype(bf16)
    saves = [copies.start(flat_ref, flat_hbm)]
    edges = dot(flat_ref[...], pick)
    load_target.wait()
    for row in range(rows):
        aim_ref[:variables, tile(row)] = target_ref[:, row, :]
    high = aim_ref[...].astype(bf16)
    low = (aim_ref[...] - high.astype(f32)).astype(bf16)
    for ref, near, second in ((first_ref, 0, 1), (last_ref, rows - 1, rows - 2)):
        ref[:channels, :cols] = flat_ref[:, tile(near)]
        ref[:channels, cols:] = flat_ref[:, tile(second)]
        ref[channels:, :cols] = high[:, tile(near)]
        ref[channels:, cols:] = low[:, tile(near)]
    saves += [copies.start(first_ref, first_hbm), copies.start(last_ref, last_hbm)]
    high_edges = dot(high, pick)
    low_edges = dot(low, pick)

    def side(begin):
        aim = jnp.concatenate([high_edges[:, begin : begin + rows], low_edges[:, begin : begin + rows]], axis=1)
        return jnp.concatenate([edges[:, begin : begin + 2 * rows], aim], axis=0)

    east, west = side(0), side(2 * rows)
    lane = lax.broadcasted_iota(jnp.int32, east.shape, 1)
    odd = lane < odd_ref[0] * LANES
    other_ref[...] = jnp.where(odd, east, west).astype(bf16)
    close_ref[...] = jnp.where(odd, west, east).astype(bf16)
    east_ref[...] = east.astype(bf16)
    west_ref[...] = west.astype(bf16)
    for ref, goal in ((other_ref, other_hbm), (close_ref, close_hbm), (east_ref, east_hbm), (west_ref, west_hbm)):
        saves.append(copies.start(ref, goal))
    for save in saves:
        save.wait()


def rim_choice(rows):
    sizes = (2 * rows,) * 4 + (HALO_LANES,) * 2
    sources = [np.zeros((size, 3 * LANES), np.float32) for size in sizes]
    left, right, east, west, north, south = sources
    for row in range(rows):
        lane = row + 2
        left[row, LANES + lane] = 1
        left[rows + row, lane] = 1
        right[row, LANES + RIM + lane] = 1
        right[rows + row, 2 * LANES + RIM + lane] = 1
        east[row, RIM + lane] = 1
        west[row, 2 * LANES + lane] = 1
    for source, lanes in ((north, (1, 0)), (south, (rows + 2, rows + 3))):
        for second, lane in enumerate(lanes):
            source[2 * LANES + second, LANES + lane] = 1
            source[2 * LANES + 2 + second, lane] = 1
            source[2 * LANES + 4 + second, LANES + RIM + lane] = 1
            source[2 * LANES + 6 + second, 2 * LANES + RIM + lane] = 1
            source[second * LANES + LANES - 1, RIM + lane] = 1
            source[second * LANES, 2 * LANES + lane] = 1
    return jnp.asarray(np.concatenate(sources), bf16)


def widen(x3_ref, place, block, before, after):
    channels = block.shape[0]
    lane = lax.broadcasted_iota(jnp.int32, (channels, LANES), 1)
    x3_ref[:channels, place] = jnp.where(lane == 0, before, pltpu.roll(block, 1, 1)).astype(bf16)
    x3_ref[channels : 2 * channels, place] = block.astype(bf16)
    x3_ref[2 * channels :, place] = jnp.where(lane == LANES - 1, after, pltpu.roll(block, LANES - 1, 1)).astype(bf16)


def activate(pre, place, b_ref, ow_ref, ob_ref, slope_ref, out_ref):
    pre = pre + b_ref[...]
    sigmoid = 1.0 / (1.0 + jnp.exp(-pre))
    active = (pre * sigmoid).astype(bf16)
    slope_ref[:, place] = sigmoid * (1.0 + pre * (1.0 - sigmoid))
    out_ref[:, place] = (dot(ow_ref[...], active) + ob_ref[...]).astype(bf16)


def inner_kernel(rows, members, x_hbm, left_hbm, right_hbm, w_hbm, b_hbm, ow_hbm, ob_hbm, all_hbm, slope_hbm, x3_hbm,
                 x_ref, left_ref, right_ref, w_ref, b_ref, ow_ref, ob_ref, out_ref, slope_ref, x3_ref, sems):
    channels = x_ref.shape[0]
    copies = Copies(sems)
    sources = (left_hbm, right_hbm, x_hbm, w_hbm, b_hbm, ow_hbm, ob_hbm)
    goals = (left_ref, right_ref, x_ref, w_ref, b_ref, ow_ref, ob_ref)
    loads = [copies.start(source, goal) for source, goal in zip(sources, goals)]
    for load in loads[:3]:
        load.wait()
    left = left_ref[:channels].astype(f32)
    right = right_ref[:channels].astype(f32)
    for row in range(rows):
        block = x_ref[:, tile(row)].astype(f32)
        widen(x3_ref, tile(row), block, left[:, row : row + 1], right[:, row : row + 1])
    saves = [copies.start(x3_ref, x3_hbm.at[:, tile(1, rows)])]
    for load in loads[3:]:
        load.wait()
    weights = w_ref[...].T
    pairs = rows // 2 - 1
    done = 0
    for stop in ((pairs + 1) // 2, pairs):
        for pair in range(done, stop):
            pre = None
            for tap_row in range(3):
                taps = weights[:, tap_row * 3 * channels : (tap_row + 1) * 3 * channels]
                term = dot(taps, x3_ref[:, tile(2 * pair + tap_row, 2)])
                pre = term if pre is None else pre + term
            activate(pre, tile(2 * pair, 2), b_ref, ow_ref, ob_ref, slope_ref, out_ref)
        lanes = tile(2 * done, 2 * (stop - done))
        goal = tile(2 * done + 2, 2 * (stop - done))
        saves.append(copies.start(slope_ref.at[:, lanes], slope_hbm.at[:, goal]))
        for member in range(members):
            saves.append(copies.start(out_ref.at[:, lanes], all_hbm.at[member, :, goal]))
        done = stop
    for save in saves:
        save.wait()


def outer_kernel(rows, members, north_ref, south_ref, odd_ref, all_in, slope_in, x3_in, other_hbm, close_hbm, left_hbm, right_hbm, east_hbm,
                 west_hbm, choice_hbm, w_hbm, b_hbm, ow_hbm, ob_hbm, all_hbm, slope_hbm, x3_hbm, truth_hbm,
                 other_ref, close_ref, left_ref, right_ref, east_ref, west_ref, choice_ref, w_ref, b_ref, ow_ref, ob_ref,
                 truth_ref, out_ref, slope_ref, near_ref, sems):
    del all_in, slope_in
    channels = slope_ref.shape[0]
    variables = out_ref.shape[0]
    copies = Copies(sems)
    loads = [
        copies.start(close_hbm, close_ref),
        copies.start(other_hbm, other_ref),
        copies.start(x3_in.at[:, tile(1, 2)], near_ref.at[:, tile(2, 2)]),
        copies.start(x3_in.at[:, tile(rows - 1, 2)], near_ref.at[:, tile(4, 2)]),
        copies.start(w_hbm, w_ref),
        copies.start(b_hbm, b_ref),
        copies.start(ow_hbm, ow_ref),
        copies.start(ob_hbm, ob_ref),
        copies.start(left_hbm, left_ref),
        copies.start(right_hbm, right_ref),
        copies.start(east_hbm, east_ref),
        copies.start(west_hbm, west_ref),
        copies.start(choice_hbm, choice_ref),
    ]
    lane3 = lax.broadcasted_iota(jnp.int32, (3 * channels, LANES), 1)
    loads[0].wait()
    loads[1].wait()
    close, other = close_ref[...].astype(f32), other_ref[...].astype(f32)
    odd = lax.broadcasted_iota(jnp.int32, close.shape, 1) < odd_ref[0] * HALO_LANES
    north, south = jnp.where(odd, close, other), jnp.where(odd, other, close)
    poles = north_ref[0], south_ref[0]
    for halo, spots in ((north, (1, 0)), (south, (6, 7))):
        halo = halo[:channels]
        for second, spot in enumerate(spots):
            before = halo[:, 2 * LANES + second : 2 * LANES + second + 1]
            after = halo[:, 2 * LANES + 4 + second : 2 * LANES + 5 + second]
            widen(near_ref, tile(spot), halo[:, tile(second)], before, after)
    for load in loads[2:8]:
        load.wait()
    saves = [
        copies.start(near_ref.at[:, tile(1)], x3_hbm.at[:, tile(0)]),
        copies.start(near_ref.at[:, tile(6)], x3_hbm.at[:, tile(rows + 1)]),
    ]
    weights = w_ref[...].T

    def taps(tap_row):
        return weights[:, tap_row * 3 * channels : (tap_row + 1) * 3 * channels]

    def beyond(above, middle, below, turned):
        pre = dot(taps(1), middle.astype(bf16))
        pre = pre + dot(taps(0), jnp.where(turned, below, above).astype(bf16))
        return pre + dot(taps(2), jnp.where(turned, above, below).astype(bf16))

    def finish(pre, place):
        activate(pre, place, b_ref, ow_ref, ob_ref, slope_ref, out_ref)

    for spot, place in ((2, 1), (5, 2)):
        pre = dot(taps(0), near_ref[:, tile(spot - 1)])
        pre = pre + dot(taps(1), near_ref[:, tile(spot)]) + dot(taps(2), near_ref[:, tile(spot + 1)])
        finish(pre, tile(place))
    for spot, place, pole in ((1, 0, poles[0]), (6, 3, poles[1])):
        above, below = near_ref[:, tile(spot - 1)].astype(f32), near_ref[:, tile(spot + 1)].astype(f32)
        finish(beyond(above, near_ref[:, tile(spot)], below, lane3 < pole * LANES), tile(place))
    for load in loads[8:]:
        load.wait()
    rim, begin = 0.0, 0
    sources = (left_ref[...], right_ref[...], east_ref[...], west_ref[...], north.astype(bf16), south.astype(bf16))
    for source in sources:
        rim = rim + dot(source, choice_ref[begin : begin + source.shape[1]])
        begin += source.shape[1]
    middle = jnp.concatenate([rim[:channels, tile(k)] for k in range(3)], axis=0)
    first = (lane3 == 1) | (lane3 == RIM + 1)
    last = (lane3 == rows + 2) | (lane3 == RIM + rows + 2)
    turned = (first & (lane3 < poles[0] * LANES)) | (last & (lane3 < poles[1] * LANES))
    finish(beyond(pltpu.roll(middle, 1, 1), middle, pltpu.roll(middle, LANES - 1, 1), turned), tile(4))
    for lanes, goal in ((tile(0, 2), tile(0, 2)), (tile(2, 3), tile(rows, 3))):
        for member in range(members):
            saves.append(copies.start(out_ref.at[:, lanes], all_hbm.at[member, :, goal]))
        saves.append(copies.start(slope_ref.at[:, lanes], slope_hbm.at[:, goal]))
    aim = slice(channels, channels + variables)
    for place, halo in ((0, north), (1, south)):
        truth_ref[:, tile(place)] = halo[aim, tile(0)] + halo[aim, tile(1)]
    side = lax.broadcasted_iota(jnp.int32, (variables, LANES), 1)
    truth_ref[:, tile(2)] = rim[aim, tile(1)] + jnp.where(side < RIM, rim[aim, tile(0)], rim[aim, tile(2)])
    saves.append(copies.start(truth_ref, truth_hbm))
    for save in saves:
        save.wait()


def weight_kernel(rows, shares, members, member_ref, all_hbm, target_hbm, truth_hbm, vw_hbm, owt_hbm, slope_hbm, x3_hbm,
                  g_hbm, term_hbm, truth_ref, vw_ref, owt_ref, g_ref, term_ref, all_ref, target_ref, out_grad_ref,
                  slope_ref, x3_ref, sems):
    channels = g_ref.shape[0]
    tiles = rows + 3
    cuts = ((0, 6), (6, 12), (12, tiles))
    copies = Copies(sems)
    first = [copies.start(vw_hbm, vw_ref), copies.start(truth_hbm, truth_ref), copies.start(target_hbm, target_ref)]
    blocks = []
    for start, stop in cuts:
        place = tile(start, stop - start)
        blocks.append(copies.start(all_hbm.at[:, :, place], all_ref.at[:, :, place]))
    later = [copies.start(owt_hbm, owt_ref), copies.start(slope_hbm, slope_ref), copies.start(x3_hbm, x3_ref)]
    for load in first:
        load.wait()

    def truth(q):
        if q == 0:
            return truth_ref[:, tile(0)]
        if q > rows:
            return truth_ref[:, tile(q - rows)]
        return target_ref[:, q - 1, :]

    for number, (start, stop) in enumerate(cuts):
        blocks[number].wait()
        for q in range(start, stop, 2):
            count = min(2, stop - q)
            place = tile(q, count)
            own = all_ref[member_ref[0], :, place].astype(f32)
            total = jnp.zeros_like(own)
            for member in range(members):
                total = total + signed(own - all_ref[member, :, place].astype(f32))
            fit = signed(own - jnp.concatenate([truth(q + n) for n in range(count)], axis=1))
            grad = vw_ref[...] * (fit / members - total / (members * (members - 1)))
            out_grad_ref[:, place] = grad.astype(bf16)
    later[0].wait()
    later[1].wait()
    for q in range(0, tiles, 2):
        place = tile(q, min(2, tiles - q))
        g_ref[:, place] = (dot(owt_ref[...], out_grad_ref[:, place]) * slope_ref[:, place]).astype(bf16)
    save = copies.start(g_ref, g_hbm)
    later[2].wait()
    grad_pre = g_ref[:, tile(1, rows)]
    terms = []
    for tap_row in range(3):
        terms.append(dot(x3_ref[:, tile(tap_row, rows)], grad_pre, (((1,), (1,)), ((), ()))))
    size = channels // shares
    pieces = []
    for quarter in TAP_QUARTERS:
        for spot in range(shares // 2):
            for share in (spot, spot + shares // 2):
                for tap in quarter:
                    begin = (tap % 3) * channels + share * size
                    pieces.append(terms[tap // 3][begin : begin + size])
                for _ in range(3 - len(quarter)):
                    pieces.append(jnp.zeros((size, channels), f32))
    term_ref[...] = jnp.concatenate(pieces, axis=0).astype(bf16)
    copies.start(term_ref, term_hbm).wait()
    save.wait()


def feature_kernel(north_ref, south_ref, g_hbm, w_hbm, out_hbm, g_ref, w_ref, out_ref, wide_ref, sems):
    channels, rows, cols = wide_ref.shape
    copies = Copies(sems)
    for load in (copies.start(g_hbm, g_ref), copies.start(w_hbm, w_ref)):
        load.wait()
    north_pole, south_pole = north_ref[0], south_ref[0]
    lane = lax.broadcasted_iota(jnp.int32, (channels, LANES), 1)

    def taps(tap_row):
        return w_ref[tap_row * 3 * channels : (tap_row + 1) * 3 * channels, :]

    def split(value, turned):
        kept = jnp.where(turned, 0.0, value)
        return kept.astype(bf16), (value - kept).astype(bf16)

    north, north_turned = split(g_ref[:, tile(0)].astype(f32), lane < north_pole * LANES)
    south, south_turned = split(g_ref[:, tile(rows + 1)].astype(f32), lane < south_pole * LANES)
    rim = g_ref[:, tile(rows + 2)].astype(f32)
    above, below = pltpu.roll(rim, 1, 1), pltpu.roll(rim, LANES - 1, 1)
    first = (lane == 2) | (lane == RIM + 2)
    last = (lane == rows + 1) | (lane == RIM + rows + 1)
    above, above_turned = split(above, first & (lane < north_pole * LANES))
    below, below_turned = split(below, last & (lane < south_pole * LANES))
    side = dot(taps(1), rim.astype(bf16))
    side = side + dot(taps(2), above) + dot(taps(0), below)
    side = side + dot(taps(0), above_turned) + dot(taps(2), below_turned)
    from_left, from_right = side[2 * channels :], side[:channels]

    for pair in range(rows // 2):
        row = 2 * pair
        upper = g_ref[:, tile(row, 2)]
        lower = g_ref[:, tile(row + 2, 2)]
        if pair == 0:
            upper = jnp.concatenate([north, g_ref[:, tile(1)]], axis=1)
        if pair == rows // 2 - 1:
            lower = jnp.concatenate([g_ref[:, tile(rows)], south], axis=1)
        spread = dot(taps(1), g_ref[:, tile(row + 1, 2)]) + dot(taps(2), upper) + dot(taps(0), lower)
        for part in range(2):
            block = spread[:, tile(part)]
            if row + part == 0:
                block = block + dot(taps(0), north_turned)
            if row + part == rows - 1:
                block = block + dot(taps(2), south_turned)
            spot = row + part + 2
            moved_west = pltpu.roll(block[:channels], LANES - 1, 1)
            moved_east = pltpu.roll(block[2 * channels :], 1, 1)
            total = block[channels : 2 * channels]
            total = total + jnp.where(lane == 0, from_left[:, spot : spot + 1], moved_east)
            total = total + jnp.where(lane == LANES - 1, from_right[:, RIM + spot : RIM + spot + 1], moved_west)
            wide_ref[:, row + part, :] = total
    out_ref[0] = wide_ref[...].astype(bf16)
    copies.start(out_ref, out_hbm).wait()


def exchange(pieces, groups):
    return lax.all_to_all(
        pieces, ("ens", "lat", "lon"), split_axis=0, concat_axis=0, axis_index_groups=groups, tiled=True
    )


def pallas(kernel, out_shape, flags, operands, scratch, copies, aliases=None, flops=0, nbytes=0):
    hbm = pl.BlockSpec(memory_space=pltpu.HBM)
    return pl.pallas_call(
        kernel,
        out_shape=out_shape,
        in_specs=[pl.BlockSpec(memory_space=pltpu.SMEM)] * len(flags) + [hbm] * len(operands),
        out_specs=(hbm,) * len(out_shape),
        scratch_shapes=[pltpu.VMEM(*spec) for spec in scratch] + [pltpu.SemaphoreType.DMA((copies,))],
        input_output_aliases=aliases or {},
        compiler_params=pltpu.CompilerParams(vmem_limit_bytes=VMEM_BYTES),
        cost_estimate=pl.CostEstimate(flops=flops, bytes_accessed=nbytes, transcendentals=0),
    )(*flags, *operands)


def like(*arrays):
    return [(array.shape, array.dtype) for array in arrays]


def on_device(features, conv_weight, conv_bias, out_weight, out_bias, var_weight, target):
    channels, rows, cols = features.shape[1:]
    variables = out_weight.shape[0]
    members = lax.axis_size("ens")
    bands, loops = lax.axis_size("lat"), lax.axis_size("lon")
    half = loops // 2
    member, band, loop = (lax.axis_index(axis) for axis in ("ens", "lat", "lon"))
    cells = rows * cols
    inner, outer = cells - 2 * cols, 5 * cols
    halo = -(-(channels + variables) // 16) * 16
    shape = jax.ShapeDtypeStruct
    odd_loop, odd_band = loop % 2 == 1, band % 2 == 1
    flags = [flag[None].astype(jnp.int32) for flag in (band == 0, band == bands - 1, odd_band)]

    close_loops = [(i, i ^ 1) for i in range(loops)]
    other_loops = [(i, (i + 1 if i % 2 else i - 1) % loops) for i in range(loops)]
    close_bands = [(b, b ^ 1) for b in range(bands)]
    other_bands = []
    for b in range(bands):
        other = b + 1 if b % 2 else b - 1
        for i in range(loops):
            goal = other * loops + i if 0 <= other < bands else b * loops + (i + half) % loops
            other_bands.append((b * loops + i, goal))

    def place(member, band, spot):
        return (member * bands + band) * loops + spot

    level_groups = [
        [place(e, b, h * half + s) for e in range(members) for s in range(half)] for b in range(bands) for h in range(2)
    ]
    column_groups = [
        [place(e, b, h * half + s) for h in range(2) for b in range(bands)] for e in range(members) for s in range(half)
    ]
    member_groups = [[place(e, b, s) for e in range(members)] for b in range(bands) for s in range(loops)]

    side, edge = shape((halo, 2 * rows), bf16), shape((halo, 2 * cols), bf16)
    prepared = (shape((channels, cells), bf16), side, side, side, side, edge, edge)
    flat, close, other, east, west, first, last = pallas(
        prepare_kernel,
        prepared,
        (odd_loop[None].astype(jnp.int32),),
        (features, target),
        [((channels, rows, cols), bf16), (target.shape, f32), ((channels, rows, cols), f32)]
        + [((halo - channels, cells), f32)] + like(*prepared),
        10,
    )
    got_close = lax.ppermute(close, "lon", close_loops)
    got_other = lax.ppermute(other, "lon", other_loops)
    left = jnp.where(~odd_loop, got_other, got_close)
    right = jnp.where(odd_loop, got_other, got_close)

    def with_corners(edge, near, second):
        picks = [side[:, k : k + 1] for side in (left, right) for k in (near, second, rows + near, rows + second)]
        return jnp.concatenate([edge] + picks + [jnp.zeros((halo, HALO_LANES - 2 * cols - 8), bf16)], axis=1)

    first = with_corners(first, 0, 1)
    last = with_corners(last, rows - 1, rows - 2)
    got_close = lax.ppermute(jnp.where(odd_band, first, last), "lat", close_bands)
    got_other = lax.ppermute(jnp.where(odd_band, last, first), ("lat", "lon"), other_bands)

    weights = conv_weight.transpose(1, 0, 2).reshape(9 * channels, channels)
    bias = (weights, conv_bias[:, None], out_weight, out_bias[:, None])
    whole = (
        shape((members, variables, inner + outer), bf16),
        shape((channels, inner + outer), f32),
        shape((3 * channels, cells + 2 * cols), bf16),
    )
    operands = (flat, left, right, *bias)
    everyone, slope, x3 = pallas(
        functools.partial(inner_kernel, rows, members),
        whole,
        (),
        operands,
        like(*operands) + [((variables, inner), bf16), ((channels, inner), f32), ((3 * channels, cells), bf16)],
        8 + 2 * (members + 1),
        flops=2 * inner * channels * (9 * channels + variables),
        nbytes=8 * 2**20,
    )
    operands = (got_other, got_close, left, right, east, west, rim_choice(rows), *bias)
    beyond = shape((variables, 3 * cols), f32)
    everyone, slope, x3, truth = pallas(
        functools.partial(outer_kernel, rows, members),
        (*whole, beyond),
        flags,
        (everyone, slope, x3, *operands),
        like(*operands, beyond)
        + [((variables, outer), bf16), ((channels, outer), f32), ((3 * channels, 8 * cols), bf16)],
        16 + 2 * (members + 1),
        aliases={3: 0, 4: 1, 5: 2},
        flops=2 * outer * channels * (9 * channels + variables),
    )
    everyone = exchange(everyone, member_groups)

    operands = (truth, var_weight[:, None], out_weight.T)
    results = (shape((channels, inner + outer), bf16), shape((12 * channels, channels), bf16))
    grads, terms = pallas(
        functools.partial(weight_kernel, rows, loops, members),
        results,
        (member[None].astype(jnp.int32),),
        (everyone, target, *operands, slope, x3),
        like(*operands, *results, everyone, target) + [((variables, inner + outer), bf16)] + like(slope, x3),
        11,
        flops=2 * cells * channels * (9 * channels + variables),
    )

    size = 3 * channels // loops
    terms = exchange(terms.reshape(members * half, 2 * size, channels), level_groups)
    terms = jnp.sum(terms.astype(f32), axis=0).astype(bf16)

    results = (shape((1, channels, rows, cols), bf16),)
    (grad_features,) = pallas(
        feature_kernel,
        results,
        flags[:2],
        (grads, weights),
        like(grads, weights, *results) + [((channels, rows, cols), f32)],
        3,
        flops=2 * cells * channels * 9 * channels,
    )

    terms = jnp.broadcast_to(terms.reshape(2, 1, size, channels), (2, bands, size, channels))
    terms = exchange(terms.reshape(2 * bands, size, channels), column_groups)
    terms = jnp.sum(terms.astype(f32), axis=0).astype(bf16)
    grad_features, terms = lax.optimization_barrier((grad_features, terms))
    terms = exchange(jnp.broadcast_to(terms, (members, size, channels)), member_groups)
    share = [terms[k, : len(quarter) * channels // loops] for k, quarter in enumerate(TAP_QUARTERS)]
    share = jnp.concatenate(share, axis=0).astype(f32)
    total_cells = members * cells * bands * loops
    grad_weight = (share / math.sqrt(total_cells)).reshape(9, channels // loops, channels).transpose(1, 0, 2)
    return grad_features, grad_weight


def solution(mesh):
    return jax.shard_map(
        on_device,
        mesh=mesh,
        in_specs=(P("ens", None, "lat", "lon"), P(), P(), P(), P(), P(), P(None, "lat", "lon")),
        out_specs=(P("ens", None, "lat", "lon"), P("lon", None, None)),
        check_vma=False,
    )
```

```python
import functools
import math

import jax
import jax.numpy as jnp
import numpy as np
from jax import lax
from jax.experimental import pallas as pl
from jax.experimental.pallas import tpu as pltpu
from jax.sharding import PartitionSpec as P

smoothing = 0.1
LANES = 128
TAP_QUARTERS = ((0, 1, 2), (3, 4), (5, 6), (7, 8))
VMEM_BYTES = 60 * 2**20
ROOMY = 50 * 10**6
FAR = 138 * 10**5
HALO_LANES = 2 * LANES + 16
RIM = 32
f32, bf16 = jnp.float32, jnp.bfloat16


def dot(a, b, dims=(((1,), (0,)), ((), ()))):
    return lax.dot_general(a, b, dims, preferred_element_type=f32)


def tile(index, count=1):
    return slice(index * LANES, (index + count) * LANES)


def signed(d):
    return d * lax.rsqrt(d * d + smoothing * smoothing)


class Copies:
    def __init__(self, sems):
        self.sems, self.made = sems, []

    def start(self, source, goal):
        copy = pltpu.make_async_copy(source, goal, self.sems.at[len(self.made)])
        copy.start()
        self.made.append(copy)
        return copy


class Plan:
    def __init__(self, channels, variables, rows):
        halo = channels + -(-variables // 16) * 16
        tall = -(-variables // 16) * 16
        self.x3 = (slice(0, 3 * channels), tile(0, rows + 2))
        top = 3 * channels
        self.flat = (slice(top, top + channels), tile(0, rows))
        top += channels
        sources = 4 * rows + LANES + 2 * HALO_LANES
        self.weights = (slice(top, top + channels), tile(0, 9))
        self.choice = (slice(top, top + sources), tile(9, 3))
        self.first = (slice(top, top + halo), tile(12, 2))
        self.last = (slice(top, top + halo), tile(14, 2))
        self.mix = (slice(top, top + tall), tile(16))
        self.mix_turned = (slice(top, top + channels), tile(17))
        self.sides = (slice(top + halo, top + 2 * halo), tile(12))
        self.rows16 = top + max(sources, 2 * halo)
        self.slope = (slice(0, channels), tile(0, rows + 3))
        self.truth = (slice(channels, channels + -(-variables // 8) * 8), tile(0, 3))
        top = channels + tall
        self.bias = (slice(top, top + LANES), tile(0))
        self.out_bias = (slice(top, top + LANES), tile(1))
        self.var_weight = (slice(top, top + LANES), tile(2))
        top += LANES
        self.aim = (slice(top, top + tall), tile(0, rows))
        self.rows32 = top + tall


def prepare_kernel(plan, odd_ref, x_hbm, target_hbm, far16, far32, close_hbm, other_hbm,
                   x_ref, target_ref, wide_ref, aim_ref, flat_ref, close_ref, other_ref, sides_ref, first_ref,
                   last_ref, sems):
    channels, rows, cols = wide_ref.shape
    variables = target_ref.shape[0]
    copies = Copies(sems)
    part = channels // 2
    halves = [slice(k * part, (k + 1) * part) for k in range(2)]
    loads = [copies.start(x_hbm.at[0, here], x_ref.at[here]) for here in halves]
    load_target = copies.start(target_hbm, target_ref)
    cell = lax.broadcasted_iota(jnp.int32, (rows * cols, 4 * rows), 0)
    slot = lax.broadcasted_iota(jnp.int32, (1, 4 * rows), 1)
    column = jnp.where(slot < rows, cols - 1, jnp.where(slot < 2 * rows, cols - 2, jnp.where(slot < 3 * rows, 0, 1)))
    pick = jnp.where(cell == (slot % rows) * cols + column, 1.0, 0.0).astype(bf16)
    aim_ref[variables - variables % 8 :] = jnp.zeros((aim_ref.shape[0] - variables + variables % 8, rows * cols), f32)
    for load, here in zip(loads, halves):
        load.wait()
        wide_ref[here] = x_ref[here].astype(f32)
        for row in range(rows):
            flat_ref[here, tile(row)] = wide_ref[here, row, :].astype(bf16)
    saves = [copies.start(flat_ref, far16.at[*plan.flat])]
    edges = dot(flat_ref[...], pick)
    load_target.wait()
    for row in range(rows):
        aim_ref[:variables, tile(row)] = target_ref[:, row, :]
    saves.append(copies.start(aim_ref, far32.at[*plan.aim]))
    high = aim_ref[...].astype(bf16)
    low = (aim_ref[...] - high.astype(f32)).astype(bf16)
    for ref, near, second in ((first_ref, 0, 1), (last_ref, rows - 1, rows - 2)):
        ref[:channels, :cols] = flat_ref[:, tile(near)]
        ref[:channels, cols:] = flat_ref[:, tile(second)]
        ref[channels:, :cols] = high[:, tile(near)]
        ref[channels:, cols:] = low[:, tile(near)]
    saves += [copies.start(first_ref, far16.at[*plan.first]), copies.start(last_ref, far16.at[*plan.last])]
    high_edges = dot(high, pick)
    low_edges = dot(low, pick)

    def side(begin):
        aim = jnp.concatenate([high_edges[:, begin : begin + rows], low_edges[:, begin : begin + rows]], axis=1)
        return jnp.concatenate([edges[:, begin : begin + 2 * rows], aim], axis=0)

    east, west = side(0), side(2 * rows)
    lane = lax.broadcasted_iota(jnp.int32, east.shape, 1)
    odd = lane < odd_ref[0] * LANES
    other_ref[...] = jnp.where(odd, east, west).astype(bf16)
    close_ref[...] = jnp.where(odd, west, east).astype(bf16)
    sides_ref[...] = jnp.zeros(sides_ref.shape, bf16)
    sides_ref[:, : 4 * rows] = jnp.concatenate([east, west], axis=1).astype(bf16)
    for ref, goal in ((other_ref, other_hbm), (close_ref, close_hbm), (sides_ref, far16.at[*plan.sides])):
        saves.append(copies.start(ref, goal))
    for save in saves:
        save.wait()


def pack_kernel(plan, far16_in, far32_in, w_hbm, choice_hbm, mix_ref, b_ref, ob_ref, vw_ref, far16, far32,
                w_ref, choice_ref, w_turned_ref, tall_ref, mix16_ref, turned_ref, row_ref, columns_ref, sems):
    del far16_in, far32_in
    variables = mix_ref.shape[0]
    copies = Copies(sems)
    load_w, load_choice = copies.start(w_hbm, w_ref), copies.start(choice_hbm, choice_ref)
    saves = []
    tall_ref[...] = jnp.zeros(tall_ref.shape, f32)
    tall_ref[:variables] = mix_ref[...].astype(f32)
    mix16_ref[...] = tall_ref[: mix16_ref.shape[0]].astype(bf16)
    turned_ref[...] = tall_ref[...].T.astype(bf16)
    saves.append(copies.start(mix16_ref, far16.at[*plan.mix]))
    saves.append(copies.start(turned_ref, far16.at[*plan.mix_turned]))
    row_ref[...] = jnp.zeros(row_ref.shape, f32)
    for number, (ref, goal) in enumerate(((b_ref, plan.bias), (ob_ref, plan.out_bias), (vw_ref, plan.var_weight))):
        row_ref[:1, : ref.shape[1]] = ref[...]
        columns_ref[number] = jnp.broadcast_to(row_ref[:1], (LANES, LANES)).T
        saves.append(copies.start(columns_ref.at[number], far32.at[*goal]))
    load_choice.wait()
    saves.append(copies.start(choice_ref, far16.at[*plan.choice]))
    load_w.wait()
    w_turned_ref[...] = w_ref[...].T
    saves.append(copies.start(w_turned_ref, far16.at[*plan.weights]))
    for save in saves:
        save.wait()


def fetch_kernel(places16, places32, far16, far32, *refs):
    copies = Copies(refs[-1])
    sources = [far16.at[*place] for place in places16] + [far32.at[*place] for place in places32]
    for load in [copies.start(source, ref) for source, ref in zip(sources, refs)]:
        load.wait()


def corner_kernel(rows, odd_loop_ref, odd_band_ref, other_ref, close_ref, first_ref, last_ref,
                  left_ref, right_ref, send_other_ref, send_close_ref):
    other, close = other_ref[...].astype(f32), close_ref[...].astype(f32)
    odd = lax.broadcasted_iota(jnp.int32, other.shape, 1) < odd_loop_ref[0] * LANES
    left = jnp.where(odd, close, other).astype(bf16)
    right = jnp.where(odd, other, close).astype(bf16)
    left_ref[...] = left
    right_ref[...] = right
    source = lax.broadcasted_iota(jnp.int32, (2 * rows, 32), 0)
    goal = lax.broadcasted_iota(jnp.int32, (2 * rows, 32), 1)
    nth, spot = goal % 4, goal % 16
    wanted = jnp.where(goal < 16, nth % 2, rows - 1 - nth % 2) + (nth // 2) * rows
    hit = source == wanted
    from_left = jnp.where(hit & (spot < 4), 1.0, 0.0).astype(bf16)
    from_right = jnp.where(hit & (spot >= 4) & (spot < 8), 1.0, 0.0).astype(bf16)
    corners = dot(left, from_left) + dot(right, from_right)
    first, last = first_ref[...].astype(f32), last_ref[...].astype(f32)
    odd_band = odd_band_ref[0] * HALO_LANES
    odd = lax.broadcasted_iota(jnp.int32, first.shape, 1) < odd_band
    send_other_ref[:, : 2 * LANES] = jnp.where(odd, last, first).astype(bf16)
    send_close_ref[:, : 2 * LANES] = jnp.where(odd, first, last).astype(bf16)
    odd = lax.broadcasted_iota(jnp.int32, (first.shape[0], 16), 1) < odd_band
    send_other_ref[:, 2 * LANES :] = jnp.where(odd, corners[:, 16:], corners[:, :16]).astype(bf16)
    send_close_ref[:, 2 * LANES :] = jnp.where(odd, corners[:, :16], corners[:, 16:]).astype(bf16)


def rim_choice(rows):
    sizes = (2 * rows,) * 2 + (LANES,) + (HALO_LANES,) * 2
    sources = [np.zeros((size, 3 * LANES), np.float32) for size in sizes]
    left, right, sides, north, south = sources
    for row in range(rows):
        lane = row + 2
        left[row, LANES + lane] = 1
        left[rows + row, lane] = 1
        right[row, LANES + RIM + lane] = 1
        right[rows + row, 2 * LANES + RIM + lane] = 1
        sides[row, RIM + lane] = 1
        sides[2 * rows + row, 2 * LANES + lane] = 1
    for source, lanes in ((north, (1, 0)), (south, (rows + 2, rows + 3))):
        for second, lane in enumerate(lanes):
            source[2 * LANES + second, LANES + lane] = 1
            source[2 * LANES + 2 + second, lane] = 1
            source[2 * LANES + 4 + second, LANES + RIM + lane] = 1
            source[2 * LANES + 6 + second, 2 * LANES + RIM + lane] = 1
            source[second * LANES + LANES - 1, RIM + lane] = 1
            source[second * LANES, 2 * LANES + lane] = 1
    return jnp.asarray(np.concatenate(sources), bf16)


def widen(x3_ref, place, block, before, after):
    channels = block.shape[0]
    lane = lax.broadcasted_iota(jnp.int32, (channels, LANES), 1)
    x3_ref[:channels, place] = jnp.where(lane == 0, before, pltpu.roll(block, 1, 1)).astype(bf16)
    x3_ref[channels : 2 * channels, place] = block.astype(bf16)
    x3_ref[2 * channels :, place] = jnp.where(lane == LANES - 1, after, pltpu.roll(block, LANES - 1, 1)).astype(bf16)


def activate(pre, place, bias, mix, out_bias, slope_ref, out_ref):
    pre = pre + bias
    sigmoid = 1.0 / (1.0 + jnp.exp(-pre))
    active = (pre * sigmoid).astype(bf16)
    slope_ref[:, place] = sigmoid * (1.0 + pre * (1.0 - sigmoid))
    out = dot(mix, active) + out_bias[: mix.shape[0]]
    out_ref[:, place] = out[: out_ref.shape[0]].astype(bf16)


def inner_kernel(rows, left_ref, right_ref, x_ref, w_ref, mix_ref, b_ref, ob_ref, out_ref, slope_ref, x3_ref):
    channels = x_ref.shape[0]
    left = left_ref[:channels].astype(f32)
    right = right_ref[:channels].astype(f32)
    for row in range(rows):
        block = x_ref[:, tile(row)].astype(f32)
        widen(x3_ref, tile(row), block, left[:, row : row + 1], right[:, row : row + 1])
    bias, out_bias = b_ref[:, :1], ob_ref[:, :1]
    for pair in range(rows // 2 - 1):
        pre = None
        for tap_row in range(3):
            taps = w_ref[:, tap_row * 3 * channels : (tap_row + 1) * 3 * channels]
            term = dot(taps, x3_ref[:, tile(2 * pair + tap_row, 2)])
            pre = term if pre is None else pre + term
        activate(pre, tile(2 * pair, 2), bias, mix_ref[...], out_bias, slope_ref, out_ref)


def outer_kernel(plan, rows, members, north_ref, south_ref, odd_ref, other_ref, close_ref, in_out_ref, in_slope_ref,
                 in_x3_ref, left_ref, right_ref, w_ref, mix_ref, choice_ref, sides_ref, b_ref, ob_ref, far16_in, far32_in,
                 all_hbm, far16, far32, truth_ref, out_ref, slope_ref, near_ref, sems):
    channels = slope_ref.shape[0]
    variables = out_ref.shape[0]
    copies = Copies(sems)
    del far16_in, far32_in
    slope_hbm, x3_hbm = far32.at[*plan.slope], far16.at[*plan.x3]
    saves = [copies.start(in_out_ref, all_hbm.at[member, :, tile(2, rows - 2)]) for member in range(members)]
    saves.append(copies.start(in_slope_ref, slope_hbm.at[:, tile(2, rows - 2)]))
    saves.append(copies.start(in_x3_ref, x3_hbm.at[:, tile(1, rows)]))
    near_ref[:, tile(2, 2)] = in_x3_ref[:, tile(0, 2)]
    near_ref[:, tile(4, 2)] = in_x3_ref[:, tile(rows - 2, 2)]
    lane3 = lax.broadcasted_iota(jnp.int32, (3 * channels, LANES), 1)
    close, other = close_ref[...].astype(f32), other_ref[...].astype(f32)
    odd = lax.broadcasted_iota(jnp.int32, close.shape, 1) < odd_ref[0] * HALO_LANES
    north, south = jnp.where(odd, close, other), jnp.where(odd, other, close)
    poles = north_ref[0], south_ref[0]
    for halo, spots in ((north, (1, 0)), (south, (6, 7))):
        halo = halo[:channels]
        for second, spot in enumerate(spots):
            before = halo[:, 2 * LANES + second : 2 * LANES + second + 1]
            after = halo[:, 2 * LANES + 4 + second : 2 * LANES + 5 + second]
            widen(near_ref, tile(spot), halo[:, tile(second)], before, after)
    saves += [
        copies.start(near_ref.at[:, tile(1)], x3_hbm.at[:, tile(0)]),
        copies.start(near_ref.at[:, tile(6)], x3_hbm.at[:, tile(rows + 1)]),
    ]
    bias, out_bias = b_ref[:, :1], ob_ref[:, :1]

    def taps(tap_row):
        return w_ref[:, tap_row * 3 * channels : (tap_row + 1) * 3 * channels]

    def beyond(above, middle, below, turned):
        pre = dot(taps(1), middle.astype(bf16))
        pre = pre + dot(taps(0), jnp.where(turned, below, above).astype(bf16))
        return pre + dot(taps(2), jnp.where(turned, above, below).astype(bf16))

    def finish(pre, place):
        activate(pre, place, bias, mix_ref[...], out_bias, slope_ref, out_ref)

    for spot, place in ((2, 1), (5, 2)):
        pre = dot(taps(0), near_ref[:, tile(spot - 1)])
        pre = pre + dot(taps(1), near_ref[:, tile(spot)]) + dot(taps(2), near_ref[:, tile(spot + 1)])
        finish(pre, tile(place))
    for spot, place, pole in ((1, 0, poles[0]), (6, 3, poles[1])):
        above, below = near_ref[:, tile(spot - 1)].astype(f32), near_ref[:, tile(spot + 1)].astype(f32)
        finish(beyond(above, near_ref[:, tile(spot)], below, lane3 < pole * LANES), tile(place))
    rim, begin = 0.0, 0
    sources = (left_ref[...], right_ref[...], sides_ref[...], north.astype(bf16), south.astype(bf16))
    for source in sources:
        rim = rim + dot(source, choice_ref[begin : begin + source.shape[1]])
        begin += source.shape[1]
    middle = jnp.concatenate([rim[:channels, tile(k)] for k in range(3)], axis=0)
    first = (lane3 == 1) | (lane3 == RIM + 1)
    last = (lane3 == rows + 2) | (lane3 == RIM + rows + 2)
    turned = (first & (lane3 < poles[0] * LANES)) | (last & (lane3 < poles[1] * LANES))
    finish(beyond(pltpu.roll(middle, 1, 1), middle, pltpu.roll(middle, LANES - 1, 1), turned), tile(4))
    for lanes, goal in ((tile(0, 2), tile(0, 2)), (tile(2, 3), tile(rows, 3))):
        for member in range(members):
            saves.append(copies.start(out_ref.at[:, lanes], all_hbm.at[member, :, goal]))
        saves.append(copies.start(slope_ref.at[:, lanes], slope_hbm.at[:, goal]))
    aim = slice(channels, channels + truth_ref.shape[0])
    for place, halo in ((0, north), (1, south)):
        truth_ref[:, tile(place)] = halo[aim, tile(0)] + halo[aim, tile(1)]
    side = lax.broadcasted_iota(jnp.int32, (truth_ref.shape[0], LANES), 1)
    truth_ref[:, tile(2)] = rim[aim, tile(1)] + jnp.where(side < RIM, rim[aim, tile(0)], rim[aim, tile(2)])
    saves.append(copies.start(truth_ref, far32.at[*plan.truth]))
    for save in saves:
        save.wait()


def weight_kernel(plan, rows, shares, members, member_ref, all_ref, far16, far32, g_hbm, term_hbm,
                  truth_ref, vw_ref, owt_ref, g_ref, term_ref, target_ref, out_grad_ref, slope_ref, x3_ref, sems):
    channels = g_ref.shape[0]
    variables = out_grad_ref.shape[0]
    tiles = rows + 3
    copies = Copies(sems)
    first = [
        copies.start(far32.at[*plan.var_weight], vw_ref),
        copies.start(far32.at[*plan.truth], truth_ref),
        copies.start(far32.at[*plan.aim], target_ref),
    ]
    later = [
        copies.start(far16.at[*plan.mix_turned], owt_ref),
        copies.start(far32.at[*plan.slope], slope_ref),
        copies.start(far16.at[*plan.x3], x3_ref),
    ]
    for load in first:
        load.wait()
    scale = vw_ref[:variables, :1]

    def truth(q):
        if q == 0:
            return truth_ref[:variables, tile(0)]
        if q > rows:
            return truth_ref[:variables, tile(q - rows)]
        return target_ref[:variables, tile(q - 1)]

    for q in range(0, tiles, 2):
        count = min(2, tiles - q)
        place = tile(q, count)
        own = all_ref[member_ref[0], :, place].astype(f32)
        total = jnp.zeros_like(own)
        for member in range(members):
            total = total + signed(own - all_ref[member, :, place].astype(f32))
        fit = signed(own - jnp.concatenate([truth(q + n) for n in range(count)], axis=1))
        grad = scale * (fit / members - total / (members * (members - 1)))
        out_grad_ref[:, place] = grad.astype(bf16)
    later[0].wait()
    later[1].wait()
    for q in range(0, tiles, 2):
        place = tile(q, min(2, tiles - q))
        g_ref[:, place] = (dot(owt_ref[:, :variables], out_grad_ref[:, place]) * slope_ref[:, place]).astype(bf16)
    save = copies.start(g_ref, g_hbm.at[:channels])
    later[2].wait()
    grad_pre = g_ref[:, tile(1, rows)]
    terms = []
    for tap_row in range(3):
        terms.append(dot(x3_ref[:, tile(tap_row, rows)], grad_pre, (((1,), (1,)), ((), ()))))
    size = channels // shares
    pieces = []
    for quarter in TAP_QUARTERS:
        for spot in range(shares // 2):
            for share in (spot, spot + shares // 2):
                for tap in quarter:
                    begin = (tap % 3) * channels + share * size
                    pieces.append(terms[tap // 3][begin : begin + size])
                for _ in range(3 - len(quarter)):
                    pieces.append(jnp.zeros((size, channels), f32))
    term_ref[...] = jnp.concatenate(pieces, axis=0).astype(bf16)
    copies.start(term_ref, term_hbm).wait()
    save.wait()


def feature_kernel(north_ref, south_ref, g_hbm, w_hbm, out_hbm, g_ref, w_ref, out_ref, wide_ref, sems):
    channels, rows, cols = wide_ref.shape
    copies = Copies(sems)
    for load in (copies.start(g_hbm.at[: g_ref.shape[0]], g_ref), copies.start(w_hbm, w_ref)):
        load.wait()
    north_pole, south_pole = north_ref[0], south_ref[0]
    lane = lax.broadcasted_iota(jnp.int32, (channels, LANES), 1)

    def taps(tap_row):
        return w_ref[tap_row * 3 * channels : (tap_row + 1) * 3 * channels, :]

    def split(value, turned):
        kept = jnp.where(turned, 0.0, value)
        return kept.astype(bf16), (value - kept).astype(bf16)

    north, north_turned = split(g_ref[:, tile(0)].astype(f32), lane < north_pole * LANES)
    south, south_turned = split(g_ref[:, tile(rows + 1)].astype(f32), lane < south_pole * LANES)
    rim = g_ref[:, tile(rows + 2)].astype(f32)
    above, below = pltpu.roll(rim, 1, 1), pltpu.roll(rim, LANES - 1, 1)
    first = (lane == 2) | (lane == RIM + 2)
    last = (lane == rows + 1) | (lane == RIM + rows + 1)
    above, above_turned = split(above, first & (lane < north_pole * LANES))
    below, below_turned = split(below, last & (lane < south_pole * LANES))
    side = dot(taps(1), rim.astype(bf16))
    side = side + dot(taps(2), above) + dot(taps(0), below)
    side = side + dot(taps(0), above_turned) + dot(taps(2), below_turned)
    from_left, from_right = side[2 * channels :], side[:channels]

    for pair in range(rows // 2):
        row = 2 * pair
        upper = g_ref[:, tile(row, 2)]
        lower = g_ref[:, tile(row + 2, 2)]
        if pair == 0:
            upper = jnp.concatenate([north, g_ref[:, tile(1)]], axis=1)
        if pair == rows // 2 - 1:
            lower = jnp.concatenate([g_ref[:, tile(rows)], south], axis=1)
        spread = dot(taps(1), g_ref[:, tile(row + 1, 2)]) + dot(taps(2), upper) + dot(taps(0), lower)
        for part in range(2):
            block = spread[:, tile(part)]
            if row + part == 0:
                block = block + dot(taps(0), north_turned)
            if row + part == rows - 1:
                block = block + dot(taps(2), south_turned)
            spot = row + part + 2
            moved_west = pltpu.roll(block[:channels], LANES - 1, 1)
            moved_east = pltpu.roll(block[2 * channels :], 1, 1)
            total = block[channels : 2 * channels]
            total = total + jnp.where(lane == 0, from_left[:, spot : spot + 1], moved_east)
            total = total + jnp.where(lane == LANES - 1, from_right[:, RIM + spot : RIM + spot + 1], moved_west)
            wide_ref[:, row + part, :] = total
    out_ref[0] = wide_ref[...].astype(bf16)
    copies.start(out_ref, out_hbm).wait()


def exchange(pieces, groups):
    return lax.all_to_all(
        pieces, ("ens", "lat", "lon"), split_axis=0, concat_axis=0, axis_index_groups=groups, tiled=True
    )


def pallas(kernel, out_shape, flags, operands, scratch, copies, outs="", vmem=VMEM_BYTES, near=(), aliases=None, flops=0, nbytes=0):
    hbm, vmem_spec = (pl.BlockSpec(memory_space=space) for space in (pltpu.HBM, pltpu.VMEM))
    return pl.pallas_call(
        kernel,
        out_shape=out_shape,
        in_specs=[pl.BlockSpec(memory_space=pltpu.SMEM)] * len(flags)
        + [vmem_spec if number in near else hbm for number in range(len(operands))],
        out_specs=tuple(vmem_spec if place == "v" else hbm for place in (outs or "h" * len(out_shape))),
        scratch_shapes=[pltpu.VMEM(*spec) for spec in scratch] + [pltpu.SemaphoreType.DMA((copies,))] * (copies > 0),
        input_output_aliases=aliases or {},
        compiler_params=pltpu.CompilerParams(vmem_limit_bytes=vmem),
        cost_estimate=pl.CostEstimate(flops=flops, bytes_accessed=nbytes, transcendentals=0),
    )(*flags, *operands)


def like(*arrays):
    return [(array.shape, array.dtype) for array in arrays]


def on_device(features, conv_weight, conv_bias, out_weight, out_bias, var_weight, target):
    channels, rows, cols = features.shape[1:]
    variables = out_weight.shape[0]
    members = lax.axis_size("ens")
    bands, loops = lax.axis_size("lat"), lax.axis_size("lon")
    half = loops // 2
    member, band, loop = (lax.axis_index(axis) for axis in ("ens", "lat", "lon"))
    cells = rows * cols
    inner, outer = cells - 2 * cols, 5 * cols
    halo = -(-(channels + variables) // 16) * 16
    shape = jax.ShapeDtypeStruct
    odd_loop, odd_band = loop % 2 == 1, band % 2 == 1
    flags = [flag[None].astype(jnp.int32) for flag in (band == 0, band == bands - 1, odd_band)]

    close_loops = [(i, i ^ 1) for i in range(loops)]
    other_loops = [(i, (i + 1 if i % 2 else i - 1) % loops) for i in range(loops)]
    close_bands = [(b, b ^ 1) for b in range(bands)]
    other_bands = []
    for b in range(bands):
        other = b + 1 if b % 2 else b - 1
        for i in range(loops):
            goal = other * loops + i if 0 <= other < bands else b * loops + (i + half) % loops
            other_bands.append((b * loops + i, goal))

    def place(member, band, spot):
        return (member * bands + band) * loops + spot

    level_groups = [
        [place(e, b, h * half + s) for e in range(members) for s in range(half)] for b in range(bands) for h in range(2)
    ]
    column_groups = [
        [place(e, b, h * half + s) for h in range(2) for b in range(bands)] for e in range(members) for s in range(half)
    ]
    member_groups = [[place(e, b, s) for e in range(members)] for b in range(bands) for s in range(loops)]

    plan = Plan(channels, variables, rows)

    def far(least, width, dtype):
        count = -(-FAR // (width * jnp.dtype(dtype).itemsize))
        return shape((-(-max(count, least) // 16) * 16, width), dtype)

    side, edge = shape((halo, 2 * rows), bf16), shape((halo, 2 * cols), bf16)
    aim = shape((halo - channels, cells), f32)
    wholes = (far(plan.rows16, cells + 2 * cols, bf16), far(plan.rows32, inner + outer, f32))
    far16, far32, close, other = pallas(
        functools.partial(prepare_kernel, plan),
        (*wholes, side, side),
        (odd_loop[None].astype(jnp.int32),),
        (features, target),
        [((channels, rows, cols), bf16), (target.shape, f32), ((channels, rows, cols), f32)]
        + like(aim) + [((channels, cells), bf16)] + like(side, side) + [((halo, LANES), bf16)] + like(edge, edge),
        10,
    )
    got_other = lax.ppermute(other, "lon", other_loops)
    got_close = lax.ppermute(close, "lon", close_loops)

    tall = halo - channels
    choice_rows = 4 * rows + LANES + 2 * HALO_LANES
    weights = conv_weight.transpose(1, 0, 2).reshape(9 * channels, channels)
    far16, far32 = pallas(
        functools.partial(pack_kernel, plan),
        wholes,
        (),
        (far16, far32, weights, rim_choice(rows), out_weight, conv_bias[None], out_bias[None], var_weight[None]),
        [(weights.shape, bf16), ((choice_rows, 3 * LANES), bf16), (weights.shape[::-1], bf16)]
        + [((LANES, LANES), f32), ((tall, LANES), bf16), ((LANES, LANES), bf16), ((8, LANES), f32)]
        + [((3, LANES, LANES), f32)],
        9,
        near=(4, 5, 6, 7),
        aliases={0: 0, 1: 1},
        nbytes=4 * 2**20,
    )
    places16 = (plan.flat, plan.weights, plan.mix, plan.choice, plan.sides, plan.first, plan.last)
    places32 = (plan.bias, plan.out_bias)
    fetched = [
        shape((place[0].stop - place[0].start, place[1].stop - place[1].start), dtype)
        for places, dtype in ((places16, bf16), (places32, f32))
        for place in places
    ]
    flat, turned, mix, choice, sides, first, last, bias, out_bias = pallas(
        functools.partial(fetch_kernel, places16, places32),
        fetched,
        (),
        (far16, far32),
        (),
        len(fetched),
        outs="v" * len(fetched),
        vmem=ROOMY,
        nbytes=4 * 2**20,
    )
    left, right, other, close = pallas(
        functools.partial(corner_kernel, rows),
        (side, side, shape((halo, HALO_LANES), bf16), shape((halo, HALO_LANES), bf16)),
        (odd_loop[None].astype(jnp.int32), flags[2]),
        (got_other, got_close, first, last),
        (),
        0,
        outs="vvvv",
        vmem=ROOMY,
        near=range(4),
    )
    got_other = lax.ppermute(other, ("lat", "lon"), other_bands)
    got_close = lax.ppermute(close, "lat", close_bands)

    inner_out, inner_slope, inner_x3 = pallas(
        functools.partial(inner_kernel, rows),
        (shape((variables, inner), bf16), shape((channels, inner), f32), shape((3 * channels, cells), bf16)),
        (),
        (left, right, flat, turned, mix, bias, out_bias),
        (),
        0,
        outs="vvv",
        vmem=ROOMY,
        near=range(7),
        flops=2 * inner * channels * (9 * channels + variables),
        nbytes=8 * 2**20,
    )
    beyond = ((-(-variables // 8) * 8, 3 * cols), f32)
    everyone, far16, far32 = pallas(
        functools.partial(outer_kernel, plan, rows, members),
        (shape((members, variables, inner + outer), bf16), *wholes),
        flags,
        (
            got_other, got_close, inner_out, inner_slope, inner_x3, left, right,
            turned, mix, choice, sides, bias, out_bias, far16, far32,
        ),
        [beyond, ((variables, outer), bf16), ((channels, outer), f32), ((3 * channels, 8 * cols), bf16)],
        5 + 4 + 2 * (members + 1),
        vmem=ROOMY,
        near=range(13),
        aliases={16: 1, 17: 2},
        flops=2 * outer * channels * (9 * channels + variables),
    )
    everyone = exchange(everyone, member_groups)

    results = (far(channels, inner + outer, bf16), shape((12 * channels, channels), bf16))
    grads_spec = ((channels, inner + outer), bf16)
    grads, terms = pallas(
        functools.partial(weight_kernel, plan, rows, loops, members),
        results,
        (member[None].astype(jnp.int32),),
        (everyone, far16, far32),
        [beyond, ((LANES, LANES), f32), ((channels, LANES), bf16), grads_spec] + like(results[1], aim)
        + [((variables, inner + outer), bf16), ((channels, inner + outer), f32)]
        + [((3 * channels, cells + 2 * cols), bf16)],
        8,
        vmem=ROOMY,
        near=(0,),
        flops=2 * cells * channels * (9 * channels + variables),
    )

    size = 3 * channels // loops
    terms = exchange(terms.reshape(members * half, 2 * size, channels), level_groups)
    terms = jnp.sum(terms.astype(f32), axis=0).astype(bf16)

    results = (shape((1, channels, rows, cols), bf16),)
    (grad_features,) = pallas(
        feature_kernel,
        results,
        flags[:2],
        (grads, weights),
        [grads_spec] + like(weights, *results) + [((channels, rows, cols), f32)],
        3,
        flops=2 * cells * channels * 9 * channels,
    )

    terms = jnp.broadcast_to(terms.reshape(2, 1, size, channels), (2, bands, size, channels))
    terms = exchange(terms.reshape(2 * bands, size, channels), column_groups)
    terms = jnp.sum(terms.astype(f32), axis=0).astype(bf16)
    grad_features, terms = lax.optimization_barrier((grad_features, terms))
    terms = exchange(jnp.broadcast_to(terms, (members, size, channels)), member_groups)
    share = [terms[k, : len(quarter) * channels // loops] for k, quarter in enumerate(TAP_QUARTERS)]
    share = jnp.concatenate(share, axis=0).astype(f32)
    total_cells = members * cells * bands * loops
    grad_weight = (share / math.sqrt(total_cells)).reshape(9, channels // loops, channels).transpose(1, 0, 2)
    return grad_features, grad_weight


def solution(mesh):
    return jax.shard_map(
        on_device,
        mesh=mesh,
        in_specs=(P("ens", None, "lat", "lon"), P(), P(), P(), P(), P(), P(None, "lat", "lon")),
        out_specs=(P("ens", None, "lat", "lon"), P("lon", None, None)),
        check_vma=False,
    )
```

```python
import functools
import math

import jax
import jax.numpy as jnp
import numpy as np
from jax import lax
from jax.experimental import pallas as pl
from jax.experimental.pallas import tpu as pltpu
from jax.sharding import PartitionSpec as P

smoothing = 0.1
LANES = 128
TAP_QUARTERS = ((0, 1, 2), (3, 4), (5, 6), (7, 8))
VMEM_BYTES = 60 * 2**20
ROOMY = 50 * 10**6
FAR = 138 * 10**5
HALO_LANES = 2 * LANES
CORNERS = 8
ACROSS = (((1,), (1,)), ((), ()))
DOWN = (((0,), (0,)), ((), ()))
RIM = 32
f32, bf16 = jnp.float32, jnp.bfloat16


def dot(a, b, dims=(((1,), (0,)), ((), ()))):
    return lax.dot_general(a, b, dims, preferred_element_type=f32)


def tile(index, count=1):
    return slice(index * LANES, (index + count) * LANES)


def signed(d):
    return d * lax.rsqrt(d * d + smoothing * smoothing)


class Copies:
    def __init__(self, sems):
        self.sems, self.made = sems, []

    def start(self, source, goal):
        copy = pltpu.make_async_copy(source, goal, self.sems.at[len(self.made)])
        copy.start()
        self.made.append(copy)
        return copy


class Plan:
    def __init__(self, channels, variables, rows):
        tall = -(-(variables + CORNERS) // 16) * 16
        halo = channels + tall
        self.x3 = (slice(0, 3 * channels), tile(0, rows + 2))
        top = 3 * channels
        self.flat = (slice(top, top + channels), tile(0, rows))
        top += channels
        sources = 4 * rows + 2 * LANES + 2 * HALO_LANES
        self.weights = (slice(top, top + channels), tile(0, 9))
        self.choice = (slice(top, top + sources), tile(9, 3))
        self.first = (slice(top, top + halo), tile(12, 2))
        self.last = (slice(top, top + halo), tile(14, 2))
        self.mix = (slice(top, top + tall), tile(16))
        self.mix_turned = (slice(top, top + channels), tile(17))
        self.sides = (slice(top + halo, top + halo + LANES), tile(12, 2))
        self.rows16 = top + max(sources, halo + LANES)
        self.slope = (slice(0, channels), tile(0, rows + 3))
        self.truth = (slice(channels, channels + -(-variables // 8) * 8), tile(0, 3))
        top = channels + tall
        self.bias = (slice(top, top + LANES), tile(0))
        self.out_bias = (slice(top, top + LANES), tile(1))
        self.var_weight = (slice(top, top + LANES), tile(2))
        top += LANES
        self.aim = (slice(top, top + tall), tile(0, rows))
        self.rows32 = top + tall


def prepare_kernel(plan, odd_ref, x_hbm, target_hbm, far16, far32, close_hbm, other_hbm,
                   x_ref, target_ref, wide_ref, aim_ref, flat_ref, close_ref, other_ref, sides_ref, first_ref,
                   last_ref, sems):
    channels, rows, cols = wide_ref.shape
    variables = target_ref.shape[0]
    copies = Copies(sems)
    part = channels // 2
    halves = [slice(k * part, (k + 1) * part) for k in range(2)]
    loads = [copies.start(x_hbm.at[0, here], x_ref.at[here]) for here in halves]
    load_target = copies.start(target_hbm, target_ref)
    cell = lax.broadcasted_iota(jnp.int32, (4 * rows, rows * cols), 1)
    slot = lax.broadcasted_iota(jnp.int32, (4 * rows, 1), 0)
    column = jnp.where(slot < rows, cols - 1, jnp.where(slot < 2 * rows, cols - 2, jnp.where(slot < 3 * rows, 0, 1)))
    pick = jnp.where(cell == (slot % rows) * cols + column, 1.0, 0.0).astype(bf16)
    aim_ref[variables - variables % 8 :] = jnp.zeros((aim_ref.shape[0] - variables + variables % 8, rows * cols), f32)
    for load, here in zip(loads, halves):
        load.wait()
        wide_ref[here] = x_ref[here].astype(f32)
        for row in range(rows):
            flat_ref[here, tile(row)] = wide_ref[here, row, :].astype(bf16)
    saves = [copies.start(flat_ref, far16.at[*plan.flat])]
    edges = dot(pick, flat_ref[...], ACROSS)
    load_target.wait()
    for row in range(rows):
        aim_ref[:variables, tile(row)] = target_ref[:, row, :]
    saves.append(copies.start(aim_ref, far32.at[*plan.aim]))
    high = aim_ref[...].astype(bf16)
    low = (aim_ref[...] - high.astype(f32)).astype(bf16)
    for ref, near, second in ((first_ref, 0, 1), (last_ref, rows - 1, rows - 2)):
        ref[:channels, :cols] = flat_ref[:, tile(near)]
        ref[:channels, cols:] = flat_ref[:, tile(second)]
        ref[channels:, :cols] = high[:, tile(near)]
        ref[channels:, cols:] = low[:, tile(near)]
    saves += [copies.start(first_ref, far16.at[*plan.first]), copies.start(last_ref, far16.at[*plan.last])]
    high_edges = dot(pick, high, ACROSS)
    low_edges = dot(pick, low, ACROSS)
    part = 2 * rows
    aims = [jnp.concatenate([high_edges[k : k + rows], low_edges[k : k + rows]], axis=0) for k in (0, part)]
    for ref in (other_ref, close_ref, sides_ref):
        ref[...] = jnp.zeros(ref.shape, bf16)
    for place, (east, west) in (
        (slice(0, channels), (edges[:part], edges[part:])),
        (slice(channels, channels + aim_ref.shape[0]), aims),
    ):
        odd = lax.broadcasted_iota(jnp.int32, east.shape, 1) < odd_ref[0] * 2 * LANES
        other_ref[:, place] = jnp.where(odd, east, west).astype(bf16)
        close_ref[:, place] = jnp.where(odd, west, east).astype(bf16)
        sides_ref[:part, place] = east.astype(bf16)
        sides_ref[part : 2 * part, place] = west.astype(bf16)
    for ref, goal in ((other_ref, other_hbm), (close_ref, close_hbm), (sides_ref, far16.at[*plan.sides])):
        saves.append(copies.start(ref, goal))
    for save in saves:
        save.wait()


def pack_kernel(plan, far16_in, far32_in, w_hbm, choice_hbm, mix_ref, b_ref, ob_ref, vw_ref, far16, far32,
                w_ref, choice_ref, w_turned_ref, tall_ref, mix16_ref, turned_ref, row_ref, columns_ref, sems):
    del far16_in, far32_in
    variables = mix_ref.shape[0]
    copies = Copies(sems)
    load_w, load_choice = copies.start(w_hbm, w_ref), copies.start(choice_hbm, choice_ref)
    saves = []
    tall_ref[...] = jnp.zeros(tall_ref.shape, f32)
    tall_ref[:variables] = mix_ref[...].astype(f32)
    mix16_ref[...] = tall_ref[: mix16_ref.shape[0]].astype(bf16)
    turned_ref[...] = tall_ref[...].T.astype(bf16)
    saves.append(copies.start(mix16_ref, far16.at[*plan.mix]))
    saves.append(copies.start(turned_ref, far16.at[*plan.mix_turned]))
    row_ref[...] = jnp.zeros(row_ref.shape, f32)
    for number, (ref, goal) in enumerate(((b_ref, plan.bias), (ob_ref, plan.out_bias), (vw_ref, plan.var_weight))):
        row_ref[:1, : ref.shape[1]] = ref[...]
        columns_ref[number] = jnp.broadcast_to(row_ref[:1], (LANES, LANES)).T
        saves.append(copies.start(columns_ref.at[number], far32.at[*goal]))
    load_choice.wait()
    saves.append(copies.start(choice_ref, far16.at[*plan.choice]))
    load_w.wait()
    w_turned_ref[...] = w_ref[...].T
    saves.append(copies.start(w_turned_ref, far16.at[*plan.weights]))
    for save in saves:
        save.wait()


def fetch_kernel(places16, places32, far16, far32, *refs):
    copies = Copies(refs[-1])
    sources = [far16.at[*place] for place in places16] + [far32.at[*place] for place in places32]
    for load in [copies.start(source, ref) for source, ref in zip(sources, refs)]:
        load.wait()


def corner_kernel(rows, odd_loop_ref, odd_band_ref, other_ref, close_ref, first_ref, last_ref,
                  left_ref, right_ref, send_other_ref, send_close_ref):
    halo = first_ref.shape[0]
    other, close = other_ref[...].astype(f32), close_ref[...].astype(f32)
    odd = lax.broadcasted_iota(jnp.int32, other.shape, 1) < odd_loop_ref[0] * 2 * LANES
    left, right = jnp.where(odd, close, other), jnp.where(odd, other, close)
    fill = jnp.zeros((LANES - 4 * rows, other.shape[1]), f32)
    turned = jnp.concatenate([left, right, fill], axis=0).T
    left_ref[...] = turned[:halo, : 2 * rows].astype(bf16)
    right_ref[...] = turned[:halo, 2 * rows : 4 * rows].astype(bf16)
    source = lax.broadcasted_iota(jnp.int32, (2 * rows, 4 * CORNERS), 0)
    goal = lax.broadcasted_iota(jnp.int32, (2 * rows, 4 * CORNERS), 1)
    nth, spot = goal % 4, goal % 16
    wanted = jnp.where(goal < 16, nth % 2, rows - 1 - nth % 2) + (nth // 2) * rows
    hit = source == wanted
    from_left = jnp.where(hit & (spot < 4), 1.0, 0.0).astype(bf16)
    from_right = jnp.where(hit & (spot >= 4) & (spot < 8), 1.0, 0.0).astype(bf16)
    corners = dot(from_left, left.astype(bf16), DOWN) + dot(from_right, right.astype(bf16), DOWN)
    of_first, of_last = corners[:CORNERS], corners[16 : 16 + CORNERS]
    first = jnp.concatenate([first_ref[...].astype(f32)[: halo - CORNERS], of_first], axis=0)
    last = jnp.concatenate([last_ref[...].astype(f32)[: halo - CORNERS], of_last], axis=0)
    odd = lax.broadcasted_iota(jnp.int32, first.shape, 1) < odd_band_ref[0] * HALO_LANES
    send_other_ref[...] = jnp.where(odd, last, first).astype(bf16)
    send_close_ref[...] = jnp.where(odd, first, last).astype(bf16)


def rim_choice(rows):
    sizes = (2 * rows,) * 2 + (LANES,) * 2 + (HALO_LANES,) * 2
    sources = [np.zeros((size, 3 * LANES), np.float32) for size in sizes]
    left, right, sides, corners, north, south = sources
    for row in range(rows):
        lane = row + 2
        left[row, LANES + lane] = 1
        left[rows + row, lane] = 1
        right[row, LANES + RIM + lane] = 1
        right[rows + row, 2 * LANES + RIM + lane] = 1
        sides[row, RIM + lane] = 1
        sides[2 * rows + row, 2 * LANES + lane] = 1
    for base, source, lanes in ((0, north, (1, 0)), (CORNERS, south, (rows + 2, rows + 3))):
        for second, lane in enumerate(lanes):
            corners[base + second, LANES + lane] = 1
            corners[base + 2 + second, lane] = 1
            corners[base + 4 + second, LANES + RIM + lane] = 1
            corners[base + 6 + second, 2 * LANES + RIM + lane] = 1
            source[second * LANES + LANES - 1, RIM + lane] = 1
            source[second * LANES, 2 * LANES + lane] = 1
    return jnp.asarray(np.concatenate(sources), bf16)


def widen(x3_ref, place, block, before, after):
    channels = block.shape[0]
    lane = lax.broadcasted_iota(jnp.int32, (channels, LANES), 1)
    x3_ref[:channels, place] = jnp.where(lane == 0, before, pltpu.roll(block, 1, 1)).astype(bf16)
    x3_ref[channels : 2 * channels, place] = block.astype(bf16)
    x3_ref[2 * channels :, place] = jnp.where(lane == LANES - 1, after, pltpu.roll(block, LANES - 1, 1)).astype(bf16)


def activate(pre, place, bias, mix, out_bias, slope_ref, out_ref):
    pre = pre + bias
    sigmoid = 1.0 / (1.0 + jnp.exp(-pre))
    active = (pre * sigmoid).astype(bf16)
    slope_ref[:, place] = sigmoid * (1.0 + pre * (1.0 - sigmoid))
    out = dot(mix, active) + out_bias[: mix.shape[0]]
    out_ref[:, place] = out[: out_ref.shape[0]].astype(bf16)


def inner_kernel(rows, left_ref, right_ref, x_ref, w_ref, mix_ref, b_ref, ob_ref, out_ref, slope_ref, x3_ref):
    channels = x_ref.shape[0]
    left = left_ref[:channels].astype(f32)
    right = right_ref[:channels].astype(f32)
    for row in range(rows):
        block = x_ref[:, tile(row)].astype(f32)
        widen(x3_ref, tile(row), block, left[:, row : row + 1], right[:, row : row + 1])
    bias, out_bias = b_ref[:, :1], ob_ref[:, :1]
    for pair in range(rows // 2 - 1):
        pre = None
        for tap_row in range(3):
            taps = w_ref[:, tap_row * 3 * channels : (tap_row + 1) * 3 * channels]
            term = dot(taps, x3_ref[:, tile(2 * pair + tap_row, 2)])
            pre = term if pre is None else pre + term
        activate(pre, tile(2 * pair, 2), bias, mix_ref[...], out_bias, slope_ref, out_ref)


def outer_kernel(plan, rows, members, north_ref, south_ref, odd_ref, other_ref, close_ref, in_out_ref, in_slope_ref,
                 in_x3_ref, left_ref, right_ref, w_ref, mix_ref, choice_ref, sides_ref, b_ref, ob_ref, far16_in, far32_in,
                 all_hbm, far16, far32, truth_ref, out_ref, slope_ref, near_ref, sems):
    channels = slope_ref.shape[0]
    variables = out_ref.shape[0]
    copies = Copies(sems)
    del far16_in, far32_in
    slope_hbm, x3_hbm = far32.at[*plan.slope], far16.at[*plan.x3]
    saves = [copies.start(in_out_ref, all_hbm.at[member, :, tile(2, rows - 2)]) for member in range(members)]
    saves.append(copies.start(in_slope_ref, slope_hbm.at[:, tile(2, rows - 2)]))
    saves.append(copies.start(in_x3_ref, x3_hbm.at[:, tile(1, rows)]))
    near_ref[:, tile(2, 2)] = in_x3_ref[:, tile(0, 2)]
    near_ref[:, tile(4, 2)] = in_x3_ref[:, tile(rows - 2, 2)]
    lane3 = lax.broadcasted_iota(jnp.int32, (3 * channels, LANES), 1)
    close, other = close_ref[...].astype(f32), other_ref[...].astype(f32)
    odd = lax.broadcasted_iota(jnp.int32, close.shape, 1) < odd_ref[0] * HALO_LANES
    north, south = jnp.where(odd, close, other), jnp.where(odd, other, close)
    poles = north_ref[0], south_ref[0]
    height = north.shape[0]
    fill = jnp.zeros((LANES - 2 * CORNERS, HALO_LANES), f32)
    corners = jnp.concatenate([north[height - CORNERS :], south[height - CORNERS :], fill], axis=0).T[:height]
    for base, halo, spots in ((0, north, (1, 0)), (CORNERS, south, (6, 7))):
        for second, spot in enumerate(spots):
            before = corners[:channels, base + second : base + second + 1]
            after = corners[:channels, base + 4 + second : base + 5 + second]
            widen(near_ref, tile(spot), halo[:channels, tile(second)], before, after)
    saves += [
        copies.start(near_ref.at[:, tile(1)], x3_hbm.at[:, tile(0)]),
        copies.start(near_ref.at[:, tile(6)], x3_hbm.at[:, tile(rows + 1)]),
    ]
    bias, out_bias = b_ref[:, :1], ob_ref[:, :1]

    def taps(tap_row):
        return w_ref[:, tap_row * 3 * channels : (tap_row + 1) * 3 * channels]

    def beyond(above, middle, below, turned):
        pre = dot(taps(1), middle.astype(bf16))
        pre = pre + dot(taps(0), jnp.where(turned, below, above).astype(bf16))
        return pre + dot(taps(2), jnp.where(turned, above, below).astype(bf16))

    def finish(pre, place):
        activate(pre, place, bias, mix_ref[...], out_bias, slope_ref, out_ref)

    for spot, place in ((2, 1), (5, 2)):
        pre = dot(taps(0), near_ref[:, tile(spot - 1)])
        pre = pre + dot(taps(1), near_ref[:, tile(spot)]) + dot(taps(2), near_ref[:, tile(spot + 1)])
        finish(pre, tile(place))
    for spot, place, pole in ((1, 0, poles[0]), (6, 3, poles[1])):
        above, below = near_ref[:, tile(spot - 1)].astype(f32), near_ref[:, tile(spot + 1)].astype(f32)
        finish(beyond(above, near_ref[:, tile(spot)], below, lane3 < pole * LANES), tile(place))
    begin = 4 * rows
    rim = dot(left_ref[...], choice_ref[: 2 * rows]) + dot(right_ref[...], choice_ref[2 * rows : begin])
    rim = rim + dot(sides_ref[...], choice_ref[begin : begin + LANES], DOWN)[:height]
    begin += LANES
    for source in (corners, north, south):
        rim = rim + dot(source.astype(bf16), choice_ref[begin : begin + source.shape[1]])
        begin += source.shape[1]
    middle = jnp.concatenate([rim[:channels, tile(k)] for k in range(3)], axis=0)
    first = (lane3 == 1) | (lane3 == RIM + 1)
    last = (lane3 == rows + 2) | (lane3 == RIM + rows + 2)
    turned = (first & (lane3 < poles[0] * LANES)) | (last & (lane3 < poles[1] * LANES))
    finish(beyond(pltpu.roll(middle, 1, 1), middle, pltpu.roll(middle, LANES - 1, 1), turned), tile(4))
    for lanes, goal in ((tile(0, 2), tile(0, 2)), (tile(2, 3), tile(rows, 3))):
        for member in range(members):
            saves.append(copies.start(out_ref.at[:, lanes], all_hbm.at[member, :, goal]))
        saves.append(copies.start(slope_ref.at[:, lanes], slope_hbm.at[:, goal]))
    aim = slice(channels, channels + truth_ref.shape[0])
    for place, halo in ((0, north), (1, south)):
        truth_ref[:, tile(place)] = halo[aim, tile(0)] + halo[aim, tile(1)]
    side = lax.broadcasted_iota(jnp.int32, (truth_ref.shape[0], LANES), 1)
    truth_ref[:, tile(2)] = rim[aim, tile(1)] + jnp.where(side < RIM, rim[aim, tile(0)], rim[aim, tile(2)])
    saves.append(copies.start(truth_ref, far32.at[*plan.truth]))
    for save in saves:
        save.wait()


def weight_kernel(plan, rows, shares, members, member_ref, all_ref, far16, far32, g_hbm, term_hbm,
                  truth_ref, vw_ref, owt_ref, g_ref, term_ref, target_ref, out_grad_ref, pair_ref, slope_ref, x3_ref, sems):
    channels = g_ref.shape[0]
    variables = out_grad_ref.shape[0]
    tiles = rows + 3
    copies = Copies(sems)
    first = [
        copies.start(far32.at[*plan.var_weight], vw_ref),
        copies.start(far32.at[*plan.truth], truth_ref),
        copies.start(far32.at[*plan.aim], target_ref),
    ]
    later = [
        copies.start(far16.at[*plan.mix_turned], owt_ref),
        copies.start(far32.at[*plan.slope], slope_ref),
        copies.start(far16.at[*plan.x3], x3_ref),
    ]
    def truth(q):
        if q == 0:
            return truth_ref[:variables, tile(0)]
        if q > rows:
            return truth_ref[:variables, tile(q - rows)]
        return target_ref[:variables, tile(q - 1)]

    blocks = [(q, min(2, tiles - q)) for q in range(0, tiles, 2)]
    for q, count in blocks:
        place = tile(q, count)
        own = all_ref[member_ref[0], :, place].astype(f32)
        total = jnp.zeros_like(own)
        for member in range(members):
            total = total + signed(own - all_ref[member, :, place].astype(f32))
        pair_ref[:, place] = total / (members * (members - 1))
    for load in first:
        load.wait()
    scale = vw_ref[:variables, :1]
    for q, count in blocks:
        place = tile(q, count)
        own = all_ref[member_ref[0], :, place].astype(f32)
        fit = signed(own - jnp.concatenate([truth(q + n) for n in range(count)], axis=1))
        out_grad_ref[:, place] = (scale * (fit / members - pair_ref[:, place])).astype(bf16)
    later[0].wait()
    later[1].wait()
    for q in range(0, tiles, 2):
        place = tile(q, min(2, tiles - q))
        g_ref[:, place] = (dot(owt_ref[:, :variables], out_grad_ref[:, place]) * slope_ref[:, place]).astype(bf16)
    save = copies.start(g_ref, g_hbm.at[:channels])
    later[2].wait()
    grad_pre = g_ref[:, tile(1, rows)]
    terms = []
    for tap_row in range(3):
        terms.append(dot(x3_ref[:, tile(tap_row, rows)], grad_pre, (((1,), (1,)), ((), ()))))
    size = channels // shares
    pieces = []
    for quarter in TAP_QUARTERS:
        for spot in range(shares // 2):
            for share in (spot, spot + shares // 2):
                for tap in quarter:
                    begin = (tap % 3) * channels + share * size
                    pieces.append(terms[tap // 3][begin : begin + size])
                for _ in range(3 - len(quarter)):
                    pieces.append(jnp.zeros((size, channels), f32))
    term_ref[...] = jnp.concatenate(pieces, axis=0).astype(bf16)
    copies.start(term_ref, term_hbm).wait()
    save.wait()


def feature_kernel(north_ref, south_ref, g_hbm, w_hbm, out_hbm, g_ref, w_ref, out_ref, wide_ref, sems):
    channels, rows, cols = wide_ref.shape
    copies = Copies(sems)
    for load in (copies.start(g_hbm.at[: g_ref.shape[0]], g_ref), copies.start(w_hbm, w_ref)):
        load.wait()
    north_pole, south_pole = north_ref[0], south_ref[0]
    lane = lax.broadcasted_iota(jnp.int32, (channels, LANES), 1)

    def taps(tap_row):
        return w_ref[tap_row * 3 * channels : (tap_row + 1) * 3 * channels, :]

    def split(value, turned):
        kept = jnp.where(turned, 0.0, value)
        return kept.astype(bf16), (value - kept).astype(bf16)

    north, north_turned = split(g_ref[:, tile(0)].astype(f32), lane < north_pole * LANES)
    south, south_turned = split(g_ref[:, tile(rows + 1)].astype(f32), lane < south_pole * LANES)
    rim = g_ref[:, tile(rows + 2)].astype(f32)
    above, below = pltpu.roll(rim, 1, 1), pltpu.roll(rim, LANES - 1, 1)
    first = (lane == 2) | (lane == RIM + 2)
    last = (lane == rows + 1) | (lane == RIM + rows + 1)
    above, above_turned = split(above, first & (lane < north_pole * LANES))
    below, below_turned = split(below, last & (lane < south_pole * LANES))
    side = dot(taps(1), rim.astype(bf16))
    side = side + dot(taps(2), above) + dot(taps(0), below)
    side = side + dot(taps(0), above_turned) + dot(taps(2), below_turned)
    from_left, from_right = side[2 * channels :], side[:channels]

    for pair in range(rows // 2):
        row = 2 * pair
        upper = g_ref[:, tile(row, 2)]
        lower = g_ref[:, tile(row + 2, 2)]
        if pair == 0:
            upper = jnp.concatenate([north, g_ref[:, tile(1)]], axis=1)
        if pair == rows // 2 - 1:
            lower = jnp.concatenate([g_ref[:, tile(rows)], south], axis=1)
        spread = dot(taps(1), g_ref[:, tile(row + 1, 2)]) + dot(taps(2), upper) + dot(taps(0), lower)
        for part in range(2):
            block = spread[:, tile(part)]
            if row + part == 0:
                block = block + dot(taps(0), north_turned)
            if row + part == rows - 1:
                block = block + dot(taps(2), south_turned)
            spot = row + part + 2
            moved_west = pltpu.roll(block[:channels], LANES - 1, 1)
            moved_east = pltpu.roll(block[2 * channels :], 1, 1)
            total = block[channels : 2 * channels]
            total = total + jnp.where(lane == 0, from_left[:, spot : spot + 1], moved_east)
            total = total + jnp.where(lane == LANES - 1, from_right[:, RIM + spot : RIM + spot + 1], moved_west)
            wide_ref[:, row + part, :] = total
    out_ref[0] = wide_ref[...].astype(bf16)
    copies.start(out_ref, out_hbm).wait()


def exchange(pieces, groups):
    return lax.all_to_all(
        pieces, ("ens", "lat", "lon"), split_axis=0, concat_axis=0, axis_index_groups=groups, tiled=True
    )


def pallas(kernel, out_shape, flags, operands, scratch, copies, outs="", vmem=VMEM_BYTES, near=(), aliases=None, flops=0, nbytes=0):
    hbm, vmem_spec = (pl.BlockSpec(memory_space=space) for space in (pltpu.HBM, pltpu.VMEM))
    return pl.pallas_call(
        kernel,
        out_shape=out_shape,
        in_specs=[pl.BlockSpec(memory_space=pltpu.SMEM)] * len(flags)
        + [vmem_spec if number in near else hbm for number in range(len(operands))],
        out_specs=tuple(vmem_spec if place == "v" else hbm for place in (outs or "h" * len(out_shape))),
        scratch_shapes=[pltpu.VMEM(*spec) for spec in scratch] + [pltpu.SemaphoreType.DMA((copies,))] * (copies > 0),
        input_output_aliases=aliases or {},
        compiler_params=pltpu.CompilerParams(vmem_limit_bytes=vmem),
        cost_estimate=pl.CostEstimate(flops=flops, bytes_accessed=nbytes, transcendentals=0),
    )(*flags, *operands)


def like(*arrays):
    return [(array.shape, array.dtype) for array in arrays]


def on_device(features, conv_weight, conv_bias, out_weight, out_bias, var_weight, target):
    channels, rows, cols = features.shape[1:]
    variables = out_weight.shape[0]
    members = lax.axis_size("ens")
    bands, loops = lax.axis_size("lat"), lax.axis_size("lon")
    half = loops // 2
    member, band, loop = (lax.axis_index(axis) for axis in ("ens", "lat", "lon"))
    cells = rows * cols
    inner, outer = cells - 2 * cols, 5 * cols
    halo = channels + -(-(variables + CORNERS) // 16) * 16
    shape = jax.ShapeDtypeStruct
    odd_loop, odd_band = loop % 2 == 1, band % 2 == 1
    flags = [flag[None].astype(jnp.int32) for flag in (band == 0, band == bands - 1, odd_band)]

    close_loops = [(i, i ^ 1) for i in range(loops)]
    other_loops = [(i, (i + 1 if i % 2 else i - 1) % loops) for i in range(loops)]
    close_bands = [(b, b ^ 1) for b in range(bands)]
    other_bands = []
    for b in range(bands):
        other = b + 1 if b % 2 else b - 1
        for i in range(loops):
            goal = other * loops + i if 0 <= other < bands else b * loops + (i + half) % loops
            other_bands.append((b * loops + i, goal))

    def place(member, band, spot):
        return (member * bands + band) * loops + spot

    level_groups = [
        [place(e, b, h * half + s) for e in range(members) for s in range(half)] for b in range(bands) for h in range(2)
    ]
    column_groups = [
        [place(e, b, h * half + s) for h in range(2) for b in range(bands)] for e in range(members) for s in range(half)
    ]
    member_groups = [[place(e, b, s) for e in range(members)] for b in range(bands) for s in range(loops)]

    plan = Plan(channels, variables, rows)

    def far(least, width, dtype):
        count = -(-FAR // (width * jnp.dtype(dtype).itemsize))
        return shape((-(-max(count, least) // 16) * 16, width), dtype)

    side, turned_side = shape((halo, 2 * rows), bf16), shape((2 * rows, 2 * LANES), bf16)
    edge, sides = shape((halo, 2 * cols), bf16), shape((LANES, 2 * LANES), bf16)
    aim = shape((halo - channels, cells), f32)
    wholes = (far(plan.rows16, cells + 2 * cols, bf16), far(plan.rows32, inner + outer, f32))
    far16, far32, close, other = pallas(
        functools.partial(prepare_kernel, plan),
        (*wholes, turned_side, turned_side),
        (odd_loop[None].astype(jnp.int32),),
        (features, target),
        [((channels, rows, cols), bf16), (target.shape, f32), ((channels, rows, cols), f32)]
        + like(aim) + [((channels, cells), bf16)] + like(turned_side, turned_side, sides, edge, edge),
        10,
    )
    got_other = lax.ppermute(other, "lon", other_loops)
    got_close = lax.ppermute(close, "lon", close_loops)

    tall = halo - channels
    choice_rows = 4 * rows + 2 * LANES + 2 * HALO_LANES
    weights = conv_weight.transpose(1, 0, 2).reshape(9 * channels, channels)
    far16, far32 = pallas(
        functools.partial(pack_kernel, plan),
        wholes,
        (),
        (far16, far32, weights, rim_choice(rows), out_weight, conv_bias[None], out_bias[None], var_weight[None]),
        [(weights.shape, bf16), ((choice_rows, 3 * LANES), bf16), (weights.shape[::-1], bf16)]
        + [((LANES, LANES), f32), ((tall, LANES), bf16), ((LANES, LANES), bf16), ((8, LANES), f32)]
        + [((3, LANES, LANES), f32)],
        9,
        near=(4, 5, 6, 7),
        aliases={0: 0, 1: 1},
        nbytes=4 * 2**20,
    )
    places16 = (plan.flat, plan.weights, plan.mix, plan.choice, plan.sides, plan.first, plan.last)
    places32 = (plan.bias, plan.out_bias)
    fetched = [
        shape((place[0].stop - place[0].start, place[1].stop - place[1].start), dtype)
        for places, dtype in ((places16, bf16), (places32, f32))
        for place in places
    ]
    flat, turned, mix, choice, sides, first, last, bias, out_bias = pallas(
        functools.partial(fetch_kernel, places16, places32),
        fetched,
        (),
        (far16, far32),
        (),
        len(fetched),
        outs="v" * len(fetched),
        vmem=ROOMY,
        nbytes=4 * 2**20,
    )
    left, right, other, close = pallas(
        functools.partial(corner_kernel, rows),
        (side, side, shape((halo, HALO_LANES), bf16), shape((halo, HALO_LANES), bf16)),
        (odd_loop[None].astype(jnp.int32), flags[2]),
        (got_other, got_close, first, last),
        (),
        0,
        outs="vvvv",
        vmem=ROOMY,
        near=range(4),
    )
    got_other = lax.ppermute(other, ("lat", "lon"), other_bands)
    got_close = lax.ppermute(close, "lat", close_bands)

    inner_out, inner_slope, inner_x3 = pallas(
        functools.partial(inner_kernel, rows),
        (shape((variables, inner), bf16), shape((channels, inner), f32), shape((3 * channels, cells), bf16)),
        (),
        (left, right, flat, turned, mix, bias, out_bias),
        (),
        0,
        outs="vvv",
        vmem=ROOMY,
        near=range(7),
        flops=2 * inner * channels * (9 * channels + variables),
        nbytes=8 * 2**20,
    )
    beyond = ((-(-variables // 8) * 8, 3 * cols), f32)
    everyone, far16, far32 = pallas(
        functools.partial(outer_kernel, plan, rows, members),
        (shape((members, variables, inner + outer), bf16), *wholes),
        flags,
        (
            got_other, got_close, inner_out, inner_slope, inner_x3, left, right,
            turned, mix, choice, sides, bias, out_bias, far16, far32,
        ),
        [beyond, ((variables, outer), bf16), ((channels, outer), f32), ((3 * channels, 8 * cols), bf16)],
        5 + 4 + 2 * (members + 1),
        vmem=ROOMY,
        near=range(13),
        aliases={16: 1, 17: 2},
        flops=2 * outer * channels * (9 * channels + variables),
    )
    everyone = exchange(everyone, member_groups)

    results = (far(channels, inner + outer, bf16), shape((12 * channels, channels), bf16))
    grads_spec = ((channels, inner + outer), bf16)
    grads, terms = pallas(
        functools.partial(weight_kernel, plan, rows, loops, members),
        results,
        (member[None].astype(jnp.int32),),
        (everyone, far16, far32),
        [beyond, ((LANES, LANES), f32), ((channels, LANES), bf16), grads_spec] + like(results[1], aim)
        + [((variables, inner + outer), bf16), ((variables, inner + outer), f32), ((channels, inner + outer), f32)]
        + [((3 * channels, cells + 2 * cols), bf16)],
        8,
        vmem=ROOMY,
        near=(0,),
        flops=2 * cells * channels * (9 * channels + variables),
    )

    size = 3 * channels // loops
    terms = exchange(terms.reshape(members * half, 2 * size, channels), level_groups)
    terms = jnp.sum(terms.astype(f32), axis=0).astype(bf16)

    results = (shape((1, channels, rows, cols), bf16),)
    (grad_features,) = pallas(
        feature_kernel,
        results,
        flags[:2],
        (grads, weights),
        [grads_spec] + like(weights, *results) + [((channels, rows, cols), f32)],
        3,
        flops=2 * cells * channels * 9 * channels,
    )

    terms = jnp.broadcast_to(terms.reshape(2, 1, size, channels), (2, bands, size, channels))
    terms = exchange(terms.reshape(2 * bands, size, channels), column_groups)
    terms = jnp.sum(terms.astype(f32), axis=0).astype(bf16)
    grad_features, terms = lax.optimization_barrier((grad_features, terms))
    terms = exchange(jnp.broadcast_to(terms, (members, size, channels)), member_groups)
    share = [terms[k, : len(quarter) * channels // loops] for k, quarter in enumerate(TAP_QUARTERS)]
    share = jnp.concatenate(share, axis=0).astype(f32)
    total_cells = members * cells * bands * loops
    grad_weight = (share / math.sqrt(total_cells)).reshape(9, channels // loops, channels).transpose(1, 0, 2)
    return grad_features, grad_weight


def solution(mesh):
    return jax.shard_map(
        on_device,
        mesh=mesh,
        in_specs=(P("ens", None, "lat", "lon"), P(), P(), P(), P(), P(), P(None, "lat", "lon")),
        out_specs=(P("ens", None, "lat", "lon"), P("lon", None, None)),
        check_vma=False,
    )
```
